256 devices in a mesh: tm: 4 (over y), dom: 64 (over z, x, core).
Axes of the slice: x: 4, y: 4, z: 8, core: 2. Of those that a mesh axis runs over, the one named last changes fastest.
Arguments:
- memory: float32 [65536, 256], P('dom'), may hold values from -8 to 8
- last_update: int32 [65536], P('dom'), may hold values from -4096 to -1
- src_row: int32 [4, 16384], P('tm', 'dom'), may hold values from 0 to 1023
- event_time: int32 [4, 16384], P('tm', 'dom'), may hold values from 0 to 4095, as said below
- dst_rows: int32 [4, 32768], P('tm', 'dom'), may hold values from 0 to 1023
- dst_slot: int32 [4, 16384], P('tm', 'dom'), may hold values from 0 to 511
- request_rows: int32 [4, 524288], P('tm', 'dom'), may hold values from 0 to 1023
- neighbour_slot: int32 [4, 10, 16384], P('tm', None, 'dom'), may hold values from 0 to 8191
- neighbour_gap: int32 [4, 10, 16384], P('tm', None, 'dom'), may hold values from 0 to 4095
- freq: float32 [256], replicated, may hold values from 0.0001 to 0.1
- phase: float32 [256], replicated, may hold values from -3.140625 to 3.140625
- w_input: bfloat16 [768, 768], replicated, may hold values from -0.21875 to 0.21875
- b_input: float32 [768], replicated, may hold values from -3 to 3
- w_hidden: bfloat16 [256, 768], replicated, may hold values from -0.375 to 0.375
- b_hidden: float32 [768], replicated, may hold values from -3 to 3
- w_query: bfloat16 [512, 256], replicated, may hold values from -0.65625 to 0.65625
- w_key: bfloat16 [512, 256], replicated, may hold values from -0.65625 to 0.65625
- w_value: bfloat16 [512, 256], replicated, may hold values from -0.25 to 0.25
- w_merge: bfloat16 [512, 256], replicated, may hold values from -0.25 to 0.25
- b_merge: float32 [256], replicated, may hold values from -3 to 3
- w_out: bfloat16 [256, 256], replicated, may hold values from -0.375 to 0.375
- b_out: float32 [256], replicated, may hold values from -3 to 3
Outputs:
- new_memory: float32 [4, 65536, 256], P('tm', 'dom')
- embedding: bfloat16 [4, 16384, 256], P('tm', 'dom')
The draws below stay inside these ranges and needn't reach their ends.
Inputs may be any that keep to these rules, and one draw needn't show every extreme that they name: `event_time`: the events of batch b have times b * 1024 to (b + 1) * 1024 - 1.
All inputs are finite; a program needn't handle non-finite values.
Results may differ from the reference program's by a relative error of at most 0.02.
Values may be sent and summed in bfloat16 or wider, within the bound.
A program may use at most 128 MiB of HBM per device.

```python
import math
import jax
import jax.numpy as jnp
import numpy as np

M = 256
TD = 256
HEADS = 4
NBR = 10
SPAN = 1024
EV_DEV = 256
NODE_DEV = 1024
EVENTS = 16384
NODES = 65536
CAP = 128
DCAP = 8
N_TM = 4
N_DOM = 64


def draw_memory(key, part):
    base = jax.random.uniform(key, (NODES, M), jnp.float32, -1.0, 1.0)
    return base


def draw_event_time(key, part):
    offset = jnp.arange(N_TM, dtype=jnp.int32)[:, None] * SPAN
    return offset + jax.random.randint(key, (N_TM, EVENTS), 0, SPAN, dtype=jnp.int32)


def set_ends(values, key, least, top_value):
    spot = [jax.random.randint(jax.random.fold_in(key, axis), (), 0, length) for axis, length in enumerate(values.shape)]
    widest = values.shape.index(max(values.shape))
    next_to = spot[:widest] + [(spot[widest] + 1) % values.shape[widest]] + spot[widest + 1:]
    return values.at[tuple(spot)].set(least).at[tuple(next_to)].set(top_value)


def rank_bounds(amount, lean):
    loads = [(1 << 20) // math.isqrt(rank ** lean) + 1 for rank in range(1, amount + 1)]
    scale = 1 + sum(loads) // (1 << 30)
    return np.cumsum(np.array([max(1, weight // scale) for weight in loads]))


def ranked(stream_key, extent, count, skew):
    grid = rank_bounds(count, skew)
    lot = jax.random.randint(jax.random.fold_in(stream_key, 1), extent, 0, int(grid[count - 1]))
    standing = jnp.searchsorted(jnp.asarray(grid, jnp.int32), lot, side="right")
    return jax.random.permutation(jax.random.fold_in(stream_key, 2), count)[standing].astype(jnp.int32)


def noise(own_key, extent, spread, most, kind=jnp.bfloat16):
    array = jax.random.normal(own_key, extent, jnp.float32) * spread
    return jnp.minimum(jnp.maximum(array, -most), most).astype(kind)


def setup_inputs(seed: int = 0) -> dict:
    key_of = jax.random.split(jax.random.key(seed), 23)
    memory = draw_memory(jax.random.fold_in(key_of[22], 71), 0)
    last_update = set_ends(jax.random.randint(key_of[1], (NODES,), -4 * SPAN, 0), jax.random.fold_in(key_of[1], 1), -4 * SPAN, -1).astype(jnp.int32)
    src_row = set_ends(ranked(key_of[2], (N_TM, EVENTS), NODE_DEV, 2), jax.random.fold_in(key_of[2], 3), 0, NODE_DEV - 1).astype(jnp.int32)
    event_time = draw_event_time(jax.random.fold_in(key_of[22], 71), 0)
    dst_rows = set_ends(jax.random.randint(key_of[4], (N_TM, N_DOM * N_DOM * DCAP), 0, NODE_DEV), jax.random.fold_in(key_of[4], 1), 0, NODE_DEV - 1).astype(jnp.int32)
    dst_slot = set_ends(jax.random.randint(key_of[5], (N_TM, EVENTS), 0, N_DOM * DCAP), jax.random.fold_in(key_of[5], 1), 0, (N_DOM * DCAP) - 1).astype(jnp.int32)
    request_rows = set_ends(jax.random.randint(key_of[6], (N_TM, N_DOM * N_DOM * CAP), 0, NODE_DEV), jax.random.fold_in(key_of[6], 1), 0, NODE_DEV - 1).astype(jnp.int32)
    neighbour_slot = set_ends(jax.random.randint(key_of[7], (N_TM, NBR, EVENTS), 0, N_DOM * CAP), jax.random.fold_in(key_of[7], 1), 0, (N_DOM * CAP) - 1).astype(jnp.int32)
    neighbour_gap = set_ends(jax.random.randint(key_of[8], (N_TM, NBR, EVENTS), 0, 4 * SPAN), jax.random.fold_in(key_of[8], 1), 0, (4 * SPAN) - 1).astype(jnp.int32)
    freq = jnp.clip(jnp.exp(jax.random.uniform(key_of[9], (TD,), jnp.float32, math.log(0.0001), math.log(0.1))), 0.0001, 0.1)
    phase = jnp.clip(jax.random.uniform(key_of[10], (TD,), jnp.float32, -3.140625, 3.140625), -3.140625, 3.140625)
    w_input = noise(key_of[11], (2 * M + TD, 3 * M), (2 * M + TD) ** -0.5, 0.21875)
    b_input = noise(key_of[12], (3 * M,), 0.5, 3.0, jnp.float32)
    w_hidden = noise(key_of[13], (M, 3 * M), M ** -0.5, 0.375)
    b_hidden = noise(key_of[14], (3 * M,), 0.5, 3.0, jnp.float32)
    w_query = noise(key_of[15], (M + TD, M), 0.11, 0.65625)
    w_key = noise(key_of[16], (M + TD, M), 0.11, 0.65625)
    w_value = noise(key_of[17], (M + TD, M), (M + TD) ** -0.5, 0.25)
    w_merge = noise(key_of[18], (2 * M, M), (2 * M) ** -0.5, 0.25)
    b_merge = noise(key_of[19], (M,), 0.5, 3.0, jnp.float32)
    w_out = noise(key_of[20], (M, M), M ** -0.5, 0.375)
    b_out = noise(key_of[21], (M,), 0.5, 3.0, jnp.float32)
    return dict(memory=memory, last_update=last_update, src_row=src_row, event_time=event_time, dst_rows=dst_rows, dst_slot=dst_slot, request_rows=request_rows, neighbour_slot=neighbour_slot, neighbour_gap=neighbour_gap, freq=freq, phase=phase, w_input=w_input, b_input=b_input, w_hidden=w_hidden, b_hidden=b_hidden, w_query=w_query, w_key=w_key, w_value=w_value, w_merge=w_merge, b_merge=b_merge, w_out=w_out, b_out=b_out)


def time_code(elapsed, freq, phase):
    return jnp.cos(elapsed.astype(jnp.float32)[..., None] * freq + phase)

def gru_cell(input_gates, current, w_hidden, b_hidden):
    width = current.shape[1]
    hidden_gates = jnp.dot(current.astype(jnp.bfloat16), w_hidden, preferred_element_type=jnp.float32) + b_hidden
    reset_gate = jax.nn.sigmoid(input_gates[:, :width] + hidden_gates[:, :width])
    update_gate = jax.nn.sigmoid(input_gates[:, width:2 * width] + hidden_gates[:, width:2 * width])
    candidate = jnp.tanh(input_gates[:, 2 * width:] + reset_gate * hidden_gates[:, 2 * width:])
    return (1.0 - update_gate) * candidate + update_gate * current

def advance(current, stamps, source, moments, target, freq, phase, w_input, b_input, w_hidden, b_hidden):
    nodes = current.shape[0]
    elapsed = moments - stamps[source]
    message = jnp.concatenate([current[source].astype(jnp.bfloat16), target.astype(jnp.bfloat16), time_code(elapsed, freq, phase).astype(jnp.bfloat16)], axis=1)
    projected = jnp.dot(message, w_input, preferred_element_type=jnp.float32)
    summed = jax.ops.segment_sum(projected, source, num_segments=nodes)
    counts = jax.ops.segment_sum(jnp.ones(source.shape, jnp.int32), source, num_segments=nodes)
    latest = jax.ops.segment_max(moments, source, num_segments=nodes)
    input_gates = summed / jnp.maximum(counts, 1).astype(jnp.float32)[:, None] + b_input
    updated = gru_cell(input_gates, current, w_hidden, b_hidden)
    touched = counts > 0
    return (jnp.where(touched[:, None], updated, current), jnp.where(touched, latest, stamps))

def attend(own_rows, neighbours, gaps, freq, phase, w_query, w_key, w_value, w_merge, b_merge, w_out, b_out):
    events, feature_width = own_rows.shape
    head_width = feature_width // HEADS
    resting = jnp.broadcast_to(time_code(jnp.zeros((1,), jnp.int32), freq, phase).astype(jnp.bfloat16), (events, phase.shape[0]))
    queries = jnp.dot(jnp.concatenate([own_rows, resting], axis=1), w_query, preferred_element_type=jnp.float32).astype(jnp.bfloat16)
    key_input = jnp.concatenate([neighbours, time_code(gaps, freq, phase).astype(jnp.bfloat16)], axis=2)
    flattened = key_input.reshape(-1, key_input.shape[-1])
    key_rows = jnp.dot(flattened, w_key, preferred_element_type=jnp.float32).astype(jnp.bfloat16)
    value_rows = jnp.dot(flattened, w_value, preferred_element_type=jnp.float32).astype(jnp.bfloat16)
    key_rows = key_rows.reshape(neighbours.shape[0], events, HEADS, head_width)
    value_rows = value_rows.reshape(neighbours.shape[0], events, HEADS, head_width)
    scores = jnp.einsum('ehd,nehd->neh', queries.reshape(events, HEADS, head_width).astype(jnp.float32), key_rows.astype(jnp.float32)) / math.sqrt(head_width)
    weights = jax.nn.softmax(scores, axis=0).astype(jnp.bfloat16)
    attended = jnp.einsum('neh,nehd->ehd', weights.astype(jnp.float32), value_rows.astype(jnp.float32))
    attended = attended.reshape(events, feature_width).astype(jnp.bfloat16)
    merged = jax.nn.relu(jnp.dot(jnp.concatenate([attended, own_rows], axis=1), w_merge, preferred_element_type=jnp.float32) + b_merge).astype(jnp.bfloat16)
    return (jnp.dot(merged, w_out, preferred_element_type=jnp.float32) + b_out).astype(jnp.bfloat16)

def reference(memory, last_update, src_row, event_time, dst_rows, dst_slot, request_rows, neighbour_slot, neighbour_gap, freq, phase, w_input, b_input, w_hidden, b_hidden, w_query, w_key, w_value, w_merge, b_merge, w_out, b_out):
    owners = jnp.arange(EVENTS, dtype=jnp.int32) // EV_DEV
    current, stamps = (memory, last_update)
    after_all = []
    embedded = []
    for period in range(N_TM):
        source = owners * NODE_DEV + src_row[period]
        target_table = dst_rows[period].reshape(N_DOM, N_DOM * DCAP)
        slots = dst_slot[period]
        target = slots // DCAP * NODE_DEV + target_table[owners, slots]
        request_table = request_rows[period].reshape(N_DOM, N_DOM * CAP)
        near_slots = neighbour_slot[period]
        near_ids = near_slots // CAP * NODE_DEV + request_table[owners[None, :], near_slots]
        rows_half = current.astype(jnp.bfloat16)
        embedded.append(attend(rows_half[source], rows_half[near_ids], neighbour_gap[period], freq, phase, w_query, w_key, w_value, w_merge, b_merge, w_out, b_out))
        current, stamps = advance(current, stamps, source, event_time[period], current[target], freq, phase, w_input, b_input, w_hidden, b_hidden)
        after_all.append(current)
    return (jnp.stack(after_all), jnp.stack(embedded))
```

```python
import functools
import math

import jax
import jax.numpy as jnp
from jax import lax
from jax.experimental import pallas as pl
from jax.experimental.pallas import tpu as pltpu
from jax.sharding import PartitionSpec as P

HEADS = 4
MESH = pl.DeviceIdType.MESH
BF = jnp.bfloat16
F32 = jnp.float32


def cosine(x):
    turns = jnp.floor(x * (0.5 / math.pi) + 0.5)
    h = 0.5 * ((x - turns * 6.28125) - turns * (2 * math.pi - 6.28125))
    q = h * h
    s = h + h * q * (
        -1 / 6 + q * (1 / 120 + q * (-1 / 5040 + q * (1 / 362880 - q * (1 / 39916800))))
    )
    return 1.0 - 2.0 * s * s


def dot(a, b):
    return jnp.dot(a, b, preferred_element_type=F32)


def as_column(row):
    lanes = lax.broadcasted_iota(jnp.int32, (128, 128), 1)
    subs = lax.broadcasted_iota(jnp.int32, (128, 128), 0)
    parts = []
    for i in range(row.shape[0]):
        wide = jnp.broadcast_to(row[i : i + 1, :].astype(F32), (128, 128))
        parts.append(jnp.sum(jnp.where(lanes == subs, wide, 0.0), axis=1, keepdims=True))
    return jnp.concatenate(parts, axis=0)


def as_row(row):
    return jnp.concatenate([row[i : i + 1, :] for i in range(row.shape[0])], axis=1)


def split(x):
    hi = x.astype(BF)
    return hi, (x - hi.astype(F32)).astype(BF)


def chain_kernel(
    periods,
    domains,
    memory,
    stamps_in,
    ints,
    freq,
    phase,
    w_input,
    b_input,
    w_hidden,
    b_hidden,
    out_memory,
    out_rows,
    cur,
    hilo,
    ibuf,
    req,
    reqr,
    gsend,
    grecv,
    ohg,
    ohs,
    oht,
    group,
    timed,
    touched,
    inverse,
    ysend_sem,
    yrecv_sem,
    rsend_sem,
    rrecv_sem,
    gsend_sem,
    grecv_sem,
):
    me_t = lax.axis_index("tm")
    me_d = lax.axis_index("dom")
    nodes, width = memory.shape
    events = ohs.shape[1]
    dcap = 8
    asked = domains * dcap
    er = events // 128

    barrier = pltpu.get_barrier_semaphore()

    def greet(i, carry):
        pl.semaphore_signal(
            barrier,
            inc=1,
            device_id={"dom": lax.rem(me_d + i, domains)},
            device_id_type=MESH,
        )
        return carry

    lax.fori_loop(1, domains, greet, 0)
    for i in range(1, periods):
        pl.semaphore_signal(
            barrier,
            inc=1,
            device_id={"tm": lax.rem(me_t + i, periods)},
            device_id_type=MESH,
        )
    pl.semaphore_wait(barrier, domains - 1 + periods - 1)

    for i in range(1, periods):
        pltpu.make_async_remote_copy(
            src_ref=ints,
            dst_ref=ibuf.at[me_t],
            send_sem=ysend_sem,
            recv_sem=yrecv_sem,
            device_id={"tm": lax.rem(me_t + i, periods)},
            device_id_type=MESH,
        ).start()
    cur[...] = memory[...]
    hi, lo = split(memory[...])
    hilo[:, :width] = hi
    hilo[:, width:] = lo
    others = ibuf.at[pl.ds(0, periods - 1)]
    pltpu.make_async_copy(others, others, yrecv_sem).wait()
    ibuf[me_t] = ints[...]

    req[...] = jnp.sum(ibuf[:, :domains, :], axis=0)[:, None, :]

    def ask(i, carry):
        peer = lax.rem(me_d + i, domains)
        pltpu.make_async_remote_copy(
            src_ref=req.at[peer],
            dst_ref=reqr.at[me_d],
            send_sem=rsend_sem,
            recv_sem=rrecv_sem,
            device_id={"dom": peer},
            device_id_type=MESH,
        ).start()
        return carry

    lax.fori_loop(1, domains, ask, 0)

    stamps = stamps_in[...].astype(F32)

    def prepare(b, stamps):
        source_rows = ibuf[b, pl.ds(domains, er), :]
        source = as_column(source_rows)
        moment = as_column(ibuf[b, pl.ds(domains + er, er), :])
        source_row = as_row(source_rows).astype(F32)
        nodes_lane = lax.broadcasted_iota(jnp.int32, (events, nodes), 1).astype(F32)
        picks = source == nodes_lane
        ohs[b] = jnp.where(picks, 1.0, 0.0).astype(BF)
        before = jnp.sum(jnp.where(picks, stamps, 0.0), axis=1, keepdims=True)
        latest = jnp.max(jnp.where(picks, moment, -1.0), axis=0, keepdims=True)
        same = source == source_row
        same_f = jnp.where(same, 1.0, 0.0)
        group[b] = same_f.astype(BF)
        inverse[b] = jnp.broadcast_to(
            1.0 / jnp.sum(same_f, axis=1, keepdims=True), inverse.shape[1:]
        )
        earlier = lax.broadcasted_iota(jnp.int32, same.shape, 0) < lax.broadcasted_iota(
            jnp.int32, same.shape, 1
        )
        first = jnp.sum(jnp.where(same & earlier, 1.0, 0.0), axis=0, keepdims=True) == 0.0
        nodes_sub = lax.broadcasted_iota(jnp.int32, (nodes, events), 0).astype(F32)
        back = jnp.where((source_row == nodes_sub) & first, 1.0, 0.0)
        oht[b] = back.astype(BF)
        touched[b] = jnp.broadcast_to(jnp.sum(back, axis=1, keepdims=True), touched.shape[1:])
        code = cosine((moment - before) * freq[...] + phase[...]).astype(BF)
        timed[b] = dot(code, w_input[2 * width :, :])
        return jnp.where(latest >= 0.0, latest, stamps)

    stamps = prepare(0, stamps)

    reqr[me_d] = req[me_d]
    rest = reqr.at[pl.ds(0, domains - 1)]
    pltpu.make_async_copy(rest, rest, rrecv_sem).wait()

    def asked_picks(b):
        wide = jnp.broadcast_to(reqr[...], (domains, dcap, 128)).reshape(asked, 128)
        lanes = lax.broadcasted_iota(jnp.int32, (asked, 128), 1)
        subs = lax.broadcasted_iota(jnp.int32, (asked, 128), 0)
        wanted = jnp.sum(
            jnp.where(lanes == b * dcap + subs % dcap, wide.astype(F32), 0.0),
            axis=1,
            keepdims=True,
        )
        lane = lax.broadcasted_iota(jnp.int32, (asked, nodes), 1).astype(F32)
        ohg[b] = jnp.where(wanted == lane, 1.0, 0.0).astype(BF)

    asked_picks(0)

    for b in range(periods):

        @pl.when(me_t == b)
        def _():
            out_rows[...] = hilo[:, :width]

        answer = dot(ohg[b], hilo[:, :width])
        answer = jnp.concatenate(
            [
                answer[:, :128].reshape(domains, dcap, 128),
                answer[:, 128:].reshape(domains, dcap, 128),
            ],
            axis=1,
        ).astype(BF)
        gsend[b] = answer

        def send(i, carry, b=b):
            peer = lax.rem(me_d + i, domains)
            pltpu.make_async_remote_copy(
                src_ref=gsend.at[b, peer],
                dst_ref=grecv.at[b, me_d],
                send_sem=gsend_sem.at[b],
                recv_sem=grecv_sem.at[b],
                device_id={"dom": peer},
                device_id_type=MESH,
            ).start()
            return carry

        lax.fori_loop(1, domains, send, 0)

        if b == 0:
            for later in range(1, periods):
                asked_picks(later)
                stamps = prepare(later, stamps)
        own = dot(ohs[b], hilo[...])
        own_hi = own[:, :width].astype(BF)
        own_f = own[:, :width] + own[:, width:]
        projected = dot(own_hi, w_input[:width, :]) + timed[b]
        hidden = dot(own_hi, w_hidden[...]) + b_hidden[...]
        slot = as_column(ibuf[b, pl.ds(domains + 2 * er, er), :]).astype(jnp.int32)
        place = (slot // dcap) * (2 * dcap) + slot % dcap
        lane = lax.broadcasted_iota(jnp.int32, (events, 2 * asked), 1)
        pick_left = jnp.where(lane == place, 1.0, 0.0).astype(BF)
        pick_right = jnp.where(lane == place + dcap, 1.0, 0.0).astype(BF)

        arrived = grecv.at[b, pl.ds(0, domains - 1)]
        pltpu.make_async_copy(arrived, arrived, grecv_sem.at[b]).wait()
        grecv[b, me_d] = gsend[b, me_d]
        fetched = grecv[b].reshape(2 * asked, 128)
        target = jnp.concatenate(
            [dot(pick_left, fetched), dot(pick_right, fetched)], axis=1
        ).astype(BF)
        projected = projected + dot(target, w_input[width : 2 * width, :])
        p_hi, p_lo = split(projected)
        gates = (dot(group[b], p_hi) + dot(group[b], p_lo)) * inverse[b][:, :1] + b_input[...]
        r = jax.nn.sigmoid(gates[:, :width] + hidden[:, :width])
        z = jax.nn.sigmoid(gates[:, width : 2 * width] + hidden[:, width : 2 * width])
        c = jnp.tanh(gates[:, 2 * width :] + r * hidden[:, 2 * width :])
        fresh = (1.0 - z) * c + z * own_f
        f_hi, f_lo = split(fresh)
        spread = dot(oht[b], jnp.concatenate([f_hi, f_lo], axis=1))
        updated = jnp.where(
            touched[b][:, :1] > 0.0, spread[:, :width] + spread[:, width:], cur[...]
        )

        @pl.when(me_t == b)
        def _():
            out_memory[...] = updated

        if b + 1 < periods:
            cur[...] = updated
            hi, lo = split(updated)
            hilo[:, :width] = hi
            hilo[:, width:] = lo

    pltpu.make_async_copy(others, others, ysend_sem).wait()
    pltpu.make_async_copy(rest, rest, rsend_sem).wait()
    for b in range(periods):
        sent = gsend.at[b, pl.ds(0, domains - 1)]
        pltpu.make_async_copy(sent, sent, gsend_sem.at[b]).wait()


def run_chain(memory, last_update, ints, freq, phase, w_input, b_input, w_hidden, b_hidden):
    periods, domains = lax.axis_size("tm"), lax.axis_size("dom")
    nodes, width = memory.shape
    er = 2
    events = er * 128
    dcap = 8
    asked = domains * dcap
    vmem = pl.BlockSpec(memory_space=pltpu.VMEM)
    return pl.pallas_call(
        functools.partial(chain_kernel, periods, domains),
        out_shape=(
            jax.ShapeDtypeStruct((nodes, width), F32),
            jax.ShapeDtypeStruct((nodes, width), BF),
        ),
        in_specs=[vmem] * 9,
        out_specs=(vmem, vmem),
        scratch_shapes=[
            pltpu.VMEM((nodes, width), F32),
            pltpu.VMEM((nodes, 2 * width), BF),
            pltpu.VMEM((periods,) + ints.shape, jnp.int32),
            pltpu.VMEM((domains, 1, 128), jnp.int32),
            pltpu.VMEM((domains, 1, 128), jnp.int32),
            pltpu.VMEM((periods, domains, 2 * dcap, 128), BF),
            pltpu.VMEM((periods, domains, 2 * dcap, 128), BF),
            pltpu.VMEM((periods, asked, nodes), BF),
            pltpu.VMEM((periods, events, nodes), BF),
            pltpu.VMEM((periods, nodes, events), BF),
            pltpu.VMEM((periods, events, events), BF),
            pltpu.VMEM((periods, events, 3 * width), F32),
            pltpu.VMEM((periods, nodes, 128), F32),
            pltpu.VMEM((periods, events, 128), F32),
            pltpu.SemaphoreType.DMA(()),
            pltpu.SemaphoreType.DMA(()),
            pltpu.SemaphoreType.DMA(()),
            pltpu.SemaphoreType.DMA(()),
            pltpu.SemaphoreType.DMA((periods,)),
            pltpu.SemaphoreType.DMA((periods,)),
        ],
        compiler_params=pltpu.CompilerParams(
            collective_id=0, has_side_effects=True, vmem_limit_bytes=48 * 2**20
        ),
        name="chain",
    )(
        memory,
        last_update[None, :],
        ints,
        freq[None, :],
        phase[None, :],
        w_input,
        b_input[None, :],
        w_hidden,
        b_hidden[None, :],
    )


def pack_integers(src_row, event_time, dst_rows, dst_slot):
    domains = lax.axis_size("dom")
    tile = jnp.tile(dst_rows[0].reshape(domains, 8), (1, 16))
    lanes = lax.broadcasted_iota(jnp.int32, tile.shape, 1)
    asks = jnp.where(lanes // 8 == lax.axis_index("tm"), tile, 0)
    rows = [a[0].reshape(-1, 128) for a in (src_row, event_time, dst_slot)]
    return jnp.concatenate([asks, *rows, jnp.zeros((2, 128), jnp.int32)], axis=0)


def time_code(elapsed, freq, phase):
    return jnp.cos(elapsed.astype(jnp.float32)[..., None] * freq + phase)


def fetch_neighbours(rows_half, wanted):
    domains = lax.axis_size("dom")

    def answer_requests(requested):
        return lax.all_to_all(rows_half[requested], "dom", split_axis=0, concat_axis=0, tiled=True)

    fetched = answer_requests(
        lax.all_to_all(wanted.reshape(domains, -1), "dom", split_axis=0, concat_axis=0, tiled=True)
    )
    return fetched.reshape(-1, rows_half.shape[1])


def attend(
    own_rows, neighbours, gaps, freq, phase, w_query, w_key, w_value, w_merge, b_merge, w_out, b_out
):
    events, feature_width = own_rows.shape
    head_width = feature_width // HEADS
    resting = jnp.broadcast_to(
        time_code(jnp.zeros((1,), jnp.int32), freq, phase).astype(jnp.bfloat16),
        (events, phase.shape[0]),
    )
    queries = jnp.dot(
        jnp.concatenate([own_rows, resting], axis=1), w_query, preferred_element_type=jnp.float32
    ).astype(jnp.bfloat16)
    key_input = jnp.concatenate(
        [neighbours, time_code(gaps, freq, phase).astype(jnp.bfloat16)], axis=2
    )
    flattened = key_input.reshape(-1, key_input.shape[-1])
    key_rows = jnp.dot(flattened, w_key, preferred_element_type=jnp.float32).astype(jnp.bfloat16)
    value_rows = jnp.dot(flattened, w_value, preferred_element_type=jnp.float32).astype(
        jnp.bfloat16
    )
    key_rows = key_rows.reshape(neighbours.shape[0], events, HEADS, head_width)
    value_rows = value_rows.reshape(neighbours.shape[0], events, HEADS, head_width)
    scores = jnp.einsum(
        "ehd,nehd->neh",
        queries.reshape(events, HEADS, head_width),
        key_rows,
        preferred_element_type=jnp.float32,
    ) / math.sqrt(head_width)
    weights = jax.nn.softmax(scores, axis=0).astype(jnp.bfloat16)
    attended = jnp.einsum("neh,nehd->ehd", weights, value_rows, preferred_element_type=jnp.float32)
    attended = attended.reshape(events, feature_width).astype(jnp.bfloat16)
    merged = jax.nn.relu(
        jnp.dot(
            jnp.concatenate([attended, own_rows], axis=1),
            w_merge,
            preferred_element_type=jnp.float32,
        )
        + b_merge
    ).astype(jnp.bfloat16)
    return (jnp.dot(merged, w_out, preferred_element_type=jnp.float32) + b_out).astype(jnp.bfloat16)


def on_device(
    memory,
    last_update,
    src_row,
    event_time,
    dst_rows,
    dst_slot,
    request_rows,
    neighbour_slot,
    neighbour_gap,
    freq,
    phase,
    w_input,
    b_input,
    w_hidden,
    b_hidden,
    w_query,
    w_key,
    w_value,
    w_merge,
    b_merge,
    w_out,
    b_out,
):
    ints = pack_integers(src_row, event_time, dst_rows, dst_slot)
    updated, rows_half = run_chain(
        memory, last_update, ints, freq, phase, w_input, b_input, w_hidden, b_hidden
    )
    fetched_rows = fetch_neighbours(rows_half, request_rows[0])
    neighbours = fetched_rows[neighbour_slot[0]]
    embedded = attend(
        rows_half[src_row[0]],
        neighbours,
        neighbour_gap[0],
        freq,
        phase,
        w_query,
        w_key,
        w_value,
        w_merge,
        b_merge,
        w_out,
        b_out,
    )
    return (updated[None], embedded[None])


def solution(mesh):
    return jax.shard_map(
        on_device,
        mesh=mesh,
        in_specs=(
            P("dom", None),
            P("dom"),
            P("tm", "dom"),
            P("tm", "dom"),
            P("tm", "dom"),
            P("tm", "dom"),
            P("tm", "dom"),
            P("tm", None, "dom"),
            P("tm", None, "dom"),
            P(),
            P(),
            P(),
            P(),
            P(),
            P(),
            P(),
            P(),
            P(),
            P(),
            P(),
            P(),
            P(),
        ),
        out_specs=(P("tm", "dom", None), P("tm", "dom", None)),
        check_vma=False,
    )
```

```python
import functools
import math

import jax
import jax.numpy as jnp
from jax import lax
from jax.experimental import pallas as pl
from jax.experimental.pallas import tpu as pltpu
from jax.sharding import PartitionSpec as P

HEADS = 4
GROUP = 8
MESH = pl.DeviceIdType.MESH
BF = jnp.bfloat16
F32 = jnp.float32


def cosine(x):
    turns = jnp.floor(x * (0.5 / math.pi) + 0.5)
    h = 0.5 * ((x - turns * 6.28125) - turns * (2 * math.pi - 6.28125))
    q = h * h
    s = h + h * q * (
        -1 / 6 + q * (1 / 120 + q * (-1 / 5040 + q * (1 / 362880 - q * (1 / 39916800))))
    )
    return 1.0 - 2.0 * s * s


def dot(a, b):
    return jnp.dot(a, b, preferred_element_type=F32)


def as_column(row):
    lanes = lax.broadcasted_iota(jnp.int32, (128, 128), 1)
    subs = lax.broadcasted_iota(jnp.int32, (128, 128), 0)
    parts = []
    for i in range(row.shape[0]):
        wide = jnp.broadcast_to(row[i : i + 1, :].astype(F32), (128, 128))
        parts.append(jnp.sum(jnp.where(lanes == subs, wide, 0.0), axis=1, keepdims=True))
    return jnp.concatenate(parts, axis=0)


def as_row(row):
    return jnp.concatenate([row[i : i + 1, :] for i in range(row.shape[0])], axis=1)


def split(x):
    hi = x.astype(BF)
    return hi, (x - hi.astype(F32)).astype(BF)


def chain_kernel(
    periods,
    domains,
    memory,
    stamps_in,
    ints,
    freq,
    phase,
    w_input,
    b_input,
    w_hidden,
    b_hidden,
    out_memory,
    out_rows,
    cur,
    hilo,
    ibuf,
    req,
    reqr,
    gsend,
    grecv,
    ohg,
    ohs,
    oht,
    group,
    timed,
    touched,
    inverse,
    ysend_sem,
    yrecv_sem,
    rsend_sem,
    rrecv_sem,
    gsend_sem,
    grecv_sem,
):
    me_t = lax.axis_index("tm")
    me_d = lax.axis_index("dom")
    nodes, width = memory.shape
    events = ohs.shape[1]
    dcap = 8
    asked = domains * dcap
    er = events // 128

    barrier = pltpu.get_barrier_semaphore()

    def greet(i, carry):
        pl.semaphore_signal(
            barrier,
            inc=1,
            device_id={"dom": lax.rem(me_d + i, domains)},
            device_id_type=MESH,
        )
        return carry

    lax.fori_loop(1, domains, greet, 0)
    for i in range(1, periods):
        pl.semaphore_signal(
            barrier,
            inc=1,
            device_id={"tm": lax.rem(me_t + i, periods)},
            device_id_type=MESH,
        )
    pl.semaphore_wait(barrier, domains - 1 + periods - 1)

    for i in range(1, periods):
        pltpu.make_async_remote_copy(
            src_ref=ints,
            dst_ref=ibuf.at[me_t],
            send_sem=ysend_sem,
            recv_sem=yrecv_sem,
            device_id={"tm": lax.rem(me_t + i, periods)},
            device_id_type=MESH,
        ).start()
    cur[...] = memory[...]
    hi, lo = split(memory[...])
    hilo[:, :width] = hi
    hilo[:, width:] = lo
    others = ibuf.at[pl.ds(0, periods - 1)]
    pltpu.make_async_copy(others, others, yrecv_sem).wait()
    ibuf[me_t] = ints[...]

    req[...] = jnp.sum(ibuf[:, :domains, :], axis=0)[:, None, :]

    def ask(i, carry):
        peer = lax.rem(me_d + i, domains)
        pltpu.make_async_remote_copy(
            src_ref=req.at[peer],
            dst_ref=reqr.at[me_d],
            send_sem=rsend_sem,
            recv_sem=rrecv_sem,
            device_id={"dom": peer},
            device_id_type=MESH,
        ).start()
        return carry

    lax.fori_loop(1, domains, ask, 0)

    stamps = stamps_in[...].astype(F32)

    def prepare(b, stamps):
        source_rows = ibuf[b, pl.ds(domains, er), :]
        source = as_column(source_rows)
        moment = as_column(ibuf[b, pl.ds(domains + er, er), :])
        source_row = as_row(source_rows).astype(F32)
        nodes_lane = lax.broadcasted_iota(jnp.int32, (events, nodes), 1).astype(F32)
        picks = source == nodes_lane
        ohs[b] = jnp.where(picks, 1.0, 0.0).astype(BF)
        before = jnp.sum(jnp.where(picks, stamps, 0.0), axis=1, keepdims=True)
        latest = jnp.max(jnp.where(picks, moment, -1.0), axis=0, keepdims=True)
        same = source == source_row
        same_f = jnp.where(same, 1.0, 0.0)
        group[b] = same_f.astype(BF)
        inverse[b] = jnp.broadcast_to(
            1.0 / jnp.sum(same_f, axis=1, keepdims=True), inverse.shape[1:]
        )
        earlier = lax.broadcasted_iota(jnp.int32, same.shape, 0) < lax.broadcasted_iota(
            jnp.int32, same.shape, 1
        )
        first = jnp.sum(jnp.where(same & earlier, 1.0, 0.0), axis=0, keepdims=True) == 0.0
        nodes_sub = lax.broadcasted_iota(jnp.int32, (nodes, events), 0).astype(F32)
        back = jnp.where((source_row == nodes_sub) & first, 1.0, 0.0)
        oht[b] = back.astype(BF)
        touched[b] = jnp.broadcast_to(jnp.sum(back, axis=1, keepdims=True), touched.shape[1:])
        code = cosine((moment - before) * freq[...] + phase[...]).astype(BF)
        timed[b] = dot(code, w_input[2 * width :, :])
        return jnp.where(latest >= 0.0, latest, stamps)

    stamps = prepare(0, stamps)

    reqr[me_d] = req[me_d]
    rest = reqr.at[pl.ds(0, domains - 1)]
    pltpu.make_async_copy(rest, rest, rrecv_sem).wait()

    def asked_picks(b):
        wide = jnp.broadcast_to(reqr[...], (domains, dcap, 128)).reshape(asked, 128)
        lanes = lax.broadcasted_iota(jnp.int32, (asked, 128), 1)
        subs = lax.broadcasted_iota(jnp.int32, (asked, 128), 0)
        wanted = jnp.sum(
            jnp.where(lanes == b * dcap + subs % dcap, wide.astype(F32), 0.0),
            axis=1,
            keepdims=True,
        )
        lane = lax.broadcasted_iota(jnp.int32, (asked, nodes), 1).astype(F32)
        ohg[b] = jnp.where(wanted == lane, 1.0, 0.0).astype(BF)

    asked_picks(0)

    for b in range(periods):

        @pl.when(me_t == b)
        def _():
            out_rows[...] = hilo[:, :width]

        answer = dot(ohg[b], hilo[:, :width])
        answer = jnp.concatenate(
            [
                answer[:, :128].reshape(domains, dcap, 128),
                answer[:, 128:].reshape(domains, dcap, 128),
            ],
            axis=1,
        ).astype(BF)
        gsend[b] = answer

        def send(i, carry, b=b):
            peer = lax.rem(me_d + i, domains)
            pltpu.make_async_remote_copy(
                src_ref=gsend.at[b, peer],
                dst_ref=grecv.at[b, me_d],
                send_sem=gsend_sem.at[b],
                recv_sem=grecv_sem.at[b],
                device_id={"dom": peer},
                device_id_type=MESH,
            ).start()
            return carry

        lax.fori_loop(1, domains, send, 0)

        if b == 0:
            for later in range(1, periods):
                asked_picks(later)
                stamps = prepare(later, stamps)
        own = dot(ohs[b], hilo[...])
        own_hi = own[:, :width].astype(BF)
        own_f = own[:, :width] + own[:, width:]
        projected = dot(own_hi, w_input[:width, :]) + timed[b]
        hidden = dot(own_hi, w_hidden[...]) + b_hidden[...]
        slot = as_column(ibuf[b, pl.ds(domains + 2 * er, er), :]).astype(jnp.int32)
        place = (slot // dcap) * (2 * dcap) + slot % dcap
        lane = lax.broadcasted_iota(jnp.int32, (events, 2 * asked), 1)
        pick_left = jnp.where(lane == place, 1.0, 0.0).astype(BF)
        pick_right = jnp.where(lane == place + dcap, 1.0, 0.0).astype(BF)

        arrived = grecv.at[b, pl.ds(0, domains - 1)]
        pltpu.make_async_copy(arrived, arrived, grecv_sem.at[b]).wait()
        grecv[b, me_d] = gsend[b, me_d]
        fetched = grecv[b].reshape(2 * asked, 128)
        target = jnp.concatenate(
            [dot(pick_left, fetched), dot(pick_right, fetched)], axis=1
        ).astype(BF)
        projected = projected + dot(target, w_input[width : 2 * width, :])
        p_hi, p_lo = split(projected)
        gates = (dot(group[b], p_hi) + dot(group[b], p_lo)) * inverse[b][:, :1] + b_input[...]
        r = jax.nn.sigmoid(gates[:, :width] + hidden[:, :width])
        z = jax.nn.sigmoid(gates[:, width : 2 * width] + hidden[:, width : 2 * width])
        c = jnp.tanh(gates[:, 2 * width :] + r * hidden[:, 2 * width :])
        fresh = (1.0 - z) * c + z * own_f
        f_hi, f_lo = split(fresh)
        spread = dot(oht[b], jnp.concatenate([f_hi, f_lo], axis=1))
        updated = jnp.where(
            touched[b][:, :1] > 0.0, spread[:, :width] + spread[:, width:], cur[...]
        )

        @pl.when(me_t == b)
        def _():
            out_memory[...] = updated

        if b + 1 < periods:
            cur[...] = updated
            hi, lo = split(updated)
            hilo[:, :width] = hi
            hilo[:, width:] = lo

    pltpu.make_async_copy(others, others, ysend_sem).wait()
    pltpu.make_async_copy(rest, rest, rsend_sem).wait()
    for b in range(periods):
        sent = gsend.at[b, pl.ds(0, domains - 1)]
        pltpu.make_async_copy(sent, sent, gsend_sem.at[b]).wait()


def run_chain(memory, last_update, ints, freq, phase, w_input, b_input, w_hidden, b_hidden):
    periods, domains = lax.axis_size("tm"), lax.axis_size("dom")
    nodes, width = memory.shape
    er = 2
    events = er * 128
    dcap = 8
    asked = domains * dcap
    vmem = pl.BlockSpec(memory_space=pltpu.VMEM)
    return pl.pallas_call(
        functools.partial(chain_kernel, periods, domains),
        out_shape=(
            jax.ShapeDtypeStruct((nodes, width), F32),
            jax.ShapeDtypeStruct((nodes, width), BF),
        ),
        in_specs=[vmem] * 9,
        out_specs=(vmem, vmem),
        scratch_shapes=[
            pltpu.VMEM((nodes, width), F32),
            pltpu.VMEM((nodes, 2 * width), BF),
            pltpu.VMEM((periods,) + ints.shape, jnp.int32),
            pltpu.VMEM((domains, 1, 128), jnp.int32),
            pltpu.VMEM((domains, 1, 128), jnp.int32),
            pltpu.VMEM((periods, domains, 2 * dcap, 128), BF),
            pltpu.VMEM((periods, domains, 2 * dcap, 128), BF),
            pltpu.VMEM((periods, asked, nodes), BF),
            pltpu.VMEM((periods, events, nodes), BF),
            pltpu.VMEM((periods, nodes, events), BF),
            pltpu.VMEM((periods, events, events), BF),
            pltpu.VMEM((periods, events, 3 * width), F32),
            pltpu.VMEM((periods, nodes, 128), F32),
            pltpu.VMEM((periods, events, 128), F32),
            pltpu.SemaphoreType.DMA(()),
            pltpu.SemaphoreType.DMA(()),
            pltpu.SemaphoreType.DMA(()),
            pltpu.SemaphoreType.DMA(()),
            pltpu.SemaphoreType.DMA((periods,)),
            pltpu.SemaphoreType.DMA((periods,)),
        ],
        compiler_params=pltpu.CompilerParams(
            collective_id=0, has_side_effects=True, vmem_limit_bytes=48 * 2**20
        ),
        name="chain",
    )(
        memory,
        last_update[None, :],
        ints,
        freq[None, :],
        phase[None, :],
        w_input,
        b_input[None, :],
        w_hidden,
        b_hidden[None, :],
    )


def pack_integers(src_row, event_time, dst_rows, dst_slot):
    domains = lax.axis_size("dom")
    tile = jnp.tile(dst_rows[0].reshape(domains, 8), (1, 16))
    lanes = lax.broadcasted_iota(jnp.int32, tile.shape, 1)
    asks = jnp.where(lanes // 8 == lax.axis_index("tm"), tile, 0)
    rows = [a[0].reshape(-1, 128) for a in (src_row, event_time, dst_slot)]
    return jnp.concatenate([asks, *rows, jnp.zeros((2, 128), jnp.int32)], axis=0)


def near_kernel(
    domains,
    rows,
    asks,
    slots,
    gaps,
    source,
    freq,
    phase,
    w_query,
    w_key,
    w_value,
    w_merge,
    b_merge,
    w_out,
    b_out,
    out,
    store,
    answers,
    arrived,
    asked,
    slot_col,
    picked,
    timed,
    scores,
    values,
    query,
    up_send,
    up_recv,
    down_send,
    down_recv,
    ask_send,
    ask_recv,
    answer_send,
    answer_recv,
):
    nz = domains // GROUP
    me = lax.axis_index("dom")
    my_z, my_j = me // GROUP, me % GROUP
    above = lax.rem(me + GROUP, domains)
    below = lax.rem(me + domains - GROUP, domains)
    nodes, width = rows.shape
    half = nodes // 2
    neighbours, events = slots.shape
    offsets = [0]
    for step in range(1, nz // 2):
        offsets += [step, -step]
    offsets += [nz // 2]

    def mate(i):
        return my_z * GROUP + lax.rem(my_j + i, GROUP)

    barrier = pltpu.get_barrier_semaphore()
    for peer in [above, below] + [mate(i) for i in range(1, GROUP)]:
        pl.semaphore_signal(barrier, inc=1, device_id={"dom": peer}, device_id_type=MESH)
    pl.semaphore_wait(barrier, GROUP + 1)

    def pass_on(step, part, up):
        origin = lax.rem(my_z + (nz - step if up else step), nz)
        span = pl.ds(part * half, half)
        src = rows.at[span] if step == 0 else store.at[origin, span]
        send, recv = (up_send, up_recv) if up else (down_send, down_recv)
        return pltpu.make_async_remote_copy(
            src_ref=src,
            dst_ref=store.at[origin, span],
            send_sem=send.at[step, part],
            recv_sem=recv.at[step, part],
            device_id={"dom": above if up else below},
            device_id_type=MESH,
        )

    def take(step, part, up):
        origin = lax.rem(my_z + (nz - step - 1 if up else step + 1), nz)
        here = store.at[origin, pl.ds(part * half, half)]
        recv = up_recv if up else down_recv
        pltpu.make_async_copy(here, here, recv.at[step, part]).wait()

    last = nz // 2 - 1

    def moves(step, part, up):
        return step < last or part == (0 if up else 1)

    for part in range(2):
        for up in (True, False):
            if moves(0, part, up):
                pass_on(0, part, up).start()

    for i in range(1, GROUP):
        peer_j = lax.rem(my_j + i, GROUP)
        pltpu.make_async_remote_copy(
            src_ref=asks.at[:, peer_j],
            dst_ref=asked.at[my_j],
            send_sem=ask_send,
            recv_sem=ask_recv,
            device_id={"dom": mate(i)},
            device_id_type=MESH,
        ).start()
    asked[my_j] = asks[:, my_j]

    src_col = as_column(source[...])
    lane = lax.broadcasted_iota(jnp.int32, (events, nodes), 1).astype(F32)
    own = dot(jnp.where(src_col == lane, 1.0, 0.0).astype(BF), rows[...]).astype(BF)
    still = jnp.broadcast_to(cosine(phase[...]).astype(BF), (events, width))
    query[...] = (dot(own, w_query[:width, :]) + dot(still, w_query[width:, :])).astype(BF)

    def prepare(k, carry):
        here = pl.ds(k * events, events)
        gap = gaps[pl.ds(k, 1), :]
        slot = slots[pl.ds(k, 1), :]
        both = [
            jnp.concatenate(
                [as_column(v[:, j * 128 : (j + 1) * 128]) for j in range(events // 128)], axis=0
            )
            for v in (gap, slot)
        ]
        code = cosine(both[0] * freq[...] + phase[...]).astype(BF)
        timed[here, :width] = dot(code, w_key[width:, :])
        timed[here, width:] = dot(code, w_value[width:, :])
        slot_col[here, :] = jnp.broadcast_to(both[1], (events, 128))
        return carry

    rest = asked.at[pl.ds(0, GROUP - 1)]
    pltpu.make_async_copy(rest, rest, ask_recv).wait()

    def answer(i):
        offset = offsets[i]
        origin = lax.rem(my_z + offset + nz, nz)
        if offset:
            step = abs(offset) - 1
            for part in range(2):
                if step < last:
                    ups = [offset < 0]
                else:
                    ups = [part == 0]
                for up in ups:
                    take(step, part, up)
                    if step < last and moves(step + 1, part, up):
                        pass_on(step + 1, part, up).start()
        lane = lax.broadcasted_iota(jnp.int32, (GROUP // 2 * 128, nodes), 1).astype(F32)
        for side in range(2):
            wanted = jnp.concatenate(
                [
                    as_column(asked[side * (GROUP // 2) + j, origin])
                    for j in range(GROUP // 2)
                ],
                axis=0,
            )
            pick = jnp.where(wanted == lane, 1.0, 0.0).astype(BF)
            block = rows[...] if offset == 0 else store[origin]
            found = dot(pick, block).astype(BF)
            answers[i, pl.ds(side * (GROUP // 2), GROUP // 2)] = found.reshape(
                GROUP // 2, 128, width
            )
        for j in range(1, GROUP):
            pltpu.make_async_remote_copy(
                src_ref=answers.at[i, lax.rem(my_j + j, GROUP)],
                dst_ref=arrived.at[i, my_j],
                send_sem=answer_send.at[i],
                recv_sem=answer_recv.at[i],
                device_id={"dom": mate(j)},
                device_id_type=MESH,
            ).start()

    def select(i):
        origin = lax.rem(my_z + offsets[i] + nz, nz)
        here = arrived.at[i, pl.ds(0, GROUP - 1)]
        pltpu.make_async_copy(here, here, answer_recv.at[i]).wait()
        arrived[i, my_j] = answers[i, my_j]
        block = arrived[i].reshape(GROUP * 128, width)
        base = origin * (GROUP * 128)

        def some(k, carry):
            here = pl.ds(k * 2 * events, 2 * events)
            lane = (
                lax.broadcasted_iota(jnp.int32, (2 * events, GROUP * 128), 1) + base
            ).astype(F32)
            wide = slot_col[here, :1]
            part = dot(jnp.where(wide == lane, 1.0, 0.0).astype(BF), block)
            if i == 0:
                picked[here, :] = part
            else:
                picked[here, :] = picked[here, :] + part
            return carry

        lax.fori_loop(0, neighbours // 2, some, 0)

    answer(0)
    lax.fori_loop(0, neighbours, prepare, 0)
    for i in range(1, nz):
        answer(i)
        select(i - 1)
    select(nz - 1)

    head = width // HEADS
    same_head = (
        lax.broadcasted_iota(jnp.int32, (width, width), 0) // head
        == lax.broadcasted_iota(jnp.int32, (width, width), 1) // head
    )
    heads = jnp.where(same_head, 1.0, 0.0).astype(BF)
    query_f = query[...].astype(F32)
    query_2 = jnp.concatenate([query_f, query_f], axis=0)

    def score(k, carry):
        here = pl.ds(k * 2 * events, 2 * events)
        near = picked[here, :].astype(BF)
        key = (dot(near, w_key[:width, :]) + timed[here, :width]).astype(BF)
        values[here, :] = (dot(near, w_value[:width, :]) + timed[here, width:]).astype(BF)
        hi, lo = split(query_2 * key.astype(F32))
        scores[here, :] = (dot(hi, heads) + dot(lo, heads)) * (1.0 / math.sqrt(head))
        return carry

    lax.fori_loop(0, neighbours // 2, score, 0)

    def slab(ref, k):
        return ref[k * events : (k + 1) * events, :]

    top = slab(scores, 0)
    for k in range(1, neighbours):
        top = jnp.maximum(top, slab(scores, k))
    total = jnp.zeros_like(top)
    for k in range(neighbours):
        raised = jnp.exp(slab(scores, k) - top)
        scores[k * events : (k + 1) * events, :] = raised
        total = total + raised
    scale = 1.0 / total
    attended = jnp.zeros_like(top)
    for k in range(neighbours):
        weight = (slab(scores, k) * scale).astype(BF).astype(F32)
        attended = attended + weight * slab(values, k).astype(F32)
    merged = dot(attended.astype(BF), w_merge[:width, :]) + dot(own, w_merge[width:, :])
    merged = jnp.maximum(merged + b_merge[...], 0.0).astype(BF)
    out[...] = (dot(merged, w_out[...]) + b_out[...]).astype(BF)

    for step in range(nz // 2):
        for part in range(2):
            for up in (True, False):
                if moves(step, part, up):
                    pass_on(step, part, up).wait_send()
    pltpu.make_async_copy(rest, rest, ask_send).wait()
    for i in range(nz):
        sent = answers.at[i, pl.ds(0, GROUP - 1)]
        pltpu.make_async_copy(sent, sent, answer_send.at[i]).wait()


def run_near(
    rows, request_rows, slots, gaps, source, freq, phase,
    w_query, w_key, w_value, w_merge, b_merge, w_out, b_out,
):
    domains = lax.axis_size("dom")
    nz = domains // GROUP
    nodes, width = rows.shape
    neighbours, events = slots.shape
    pairs = neighbours * events
    vmem = pl.BlockSpec(memory_space=pltpu.VMEM)
    return pl.pallas_call(
        functools.partial(near_kernel, domains),
        out_shape=jax.ShapeDtypeStruct((events, width), BF),
        in_specs=[vmem] * 14,
        out_specs=vmem,
        scratch_shapes=[
            pltpu.VMEM((nz, nodes, width), BF),
            pltpu.VMEM((nz, GROUP, 128, width), BF),
            pltpu.VMEM((nz, GROUP, 128, width), BF),
            pltpu.VMEM((GROUP, nz, 1, 128), jnp.int32),
            pltpu.VMEM((pairs, 128), F32),
            pltpu.VMEM((pairs, width), F32),
            pltpu.VMEM((pairs, 2 * width), F32),
            pltpu.VMEM((pairs, width), F32),
            pltpu.VMEM((pairs, width), BF),
            pltpu.VMEM((events, width), BF),
            pltpu.SemaphoreType.DMA((nz // 2, 2)),
            pltpu.SemaphoreType.DMA((nz // 2, 2)),
            pltpu.SemaphoreType.DMA((nz // 2, 2)),
            pltpu.SemaphoreType.DMA((nz // 2, 2)),
            pltpu.SemaphoreType.DMA(()),
            pltpu.SemaphoreType.DMA(()),
            pltpu.SemaphoreType.DMA((nz,)),
            pltpu.SemaphoreType.DMA((nz,)),
        ],
        compiler_params=pltpu.CompilerParams(
            collective_id=1, has_side_effects=True, vmem_limit_bytes=48 * 2**20
        ),
        name="near",
    )(
        rows,
        request_rows.reshape(nz, GROUP, 1, 128),
        slots,
        gaps,
        source.reshape(-1, 128),
        freq[None, :],
        phase[None, :],
        w_query,
        w_key,
        w_value,
        w_merge,
        b_merge[None, :],
        w_out,
        b_out[None, :],
    )


def on_device(
    memory,
    last_update,
    src_row,
    event_time,
    dst_rows,
    dst_slot,
    request_rows,
    neighbour_slot,
    neighbour_gap,
    freq,
    phase,
    w_input,
    b_input,
    w_hidden,
    b_hidden,
    w_query,
    w_key,
    w_value,
    w_merge,
    b_merge,
    w_out,
    b_out,
):
    ints = pack_integers(src_row, event_time, dst_rows, dst_slot)
    updated, rows_half = run_chain(
        memory, last_update, ints, freq, phase, w_input, b_input, w_hidden, b_hidden
    )
    embedded = run_near(
        rows_half,
        request_rows[0],
        neighbour_slot[0],
        neighbour_gap[0],
        src_row[0],
        freq,
        phase,
        w_query,
        w_key,
        w_value,
        w_merge,
        b_merge,
        w_out,
        b_out,
    )
    return (updated[None], embedded[None])


def solution(mesh):
    return jax.shard_map(
        on_device,
        mesh=mesh,
        in_specs=(
            P("dom", None),
            P("dom"),
            P("tm", "dom"),
            P("tm", "dom"),
            P("tm", "dom"),
            P("tm", "dom"),
            P("tm", "dom"),
            P("tm", None, "dom"),
            P("tm", None, "dom"),
            P(),
            P(),
            P(),
            P(),
            P(),
            P(),
            P(),
            P(),
            P(),
            P(),
            P(),
            P(),
            P(),
        ),
        out_specs=(P("tm", "dom", None), P("tm", "dom", None)),
        check_vma=False,
    )
```

```python
import functools
import math

import jax
import jax.numpy as jnp
from jax import lax
from jax.experimental import pallas as pl
from jax.experimental.pallas import tpu as pltpu
from jax.sharding import PartitionSpec as P

HEADS = 4
GROUP = 8
DCAP = 8
CAP = 128
HALVES = 2
MESH = pl.DeviceIdType.MESH
BF = jnp.bfloat16
F32 = jnp.float32


def cosine(x):
    turns = jnp.floor(x * (0.5 / math.pi) + 0.5)
    h = 0.5 * ((x - turns * 6.28125) - turns * (2 * math.pi - 6.28125))
    q = h * h
    s = h + h * q * (
        -1 / 6 + q * (1 / 120 + q * (-1 / 5040 + q * (1 / 362880 - q * (1 / 39916800))))
    )
    return 1.0 - 2.0 * s * s


def dot(a, b):
    return jnp.dot(a, b, preferred_element_type=F32)


def as_column(row):
    lanes = lax.broadcasted_iota(jnp.int32, (128, 128), 1)
    subs = lax.broadcasted_iota(jnp.int32, (128, 128), 0)
    parts = []
    for i in range(row.shape[0]):
        wide = jnp.broadcast_to(row[i : i + 1, :].astype(F32), (128, 128))
        parts.append(jnp.sum(jnp.where(lanes == subs, wide, 0.0), axis=1, keepdims=True))
    return jnp.concatenate(parts, axis=0)


def as_row(row):
    return jnp.concatenate([row[i : i + 1, :] for i in range(row.shape[0])], axis=1)


def split(x):
    hi = x.astype(BF)
    return hi, (x - hi.astype(F32)).astype(BF)


def two_level(column):
    rest = jnp.floor(column * (1 / 128))
    lanes = lax.broadcasted_iota(jnp.int32, (column.shape[0], 128), 1).astype(F32)
    ones = jnp.where(column - rest * 128 == lanes, 1.0, 0.0).astype(BF)
    return ones, jnp.broadcast_to(rest, ones.shape).astype(BF)


def picks_of(ones, rest, first, count):
    none = jnp.zeros_like(ones)
    return jnp.concatenate(
        [jnp.where(rest == first + jnp.bfloat16(t), ones, none) for t in range(count)], axis=1
    )


def start_copy(src, dst, send_sem, recv_sem, device_id):
    copy = pltpu.make_async_remote_copy(
        src_ref=src,
        dst_ref=dst,
        send_sem=send_sem,
        recv_sem=recv_sem,
        device_id=device_id,
        device_id_type=MESH,
    )
    copy.start()


def wait_bytes(ref, sem):
    pltpu.make_async_copy(ref, ref, sem).wait()


def whole_kernel(periods, domains, *refs):
    inputs, (out_memory, out), scratch = refs[:22], refs[22:24], refs[24:]
    staged = scratch[:22]
    (
        cur,
        stamps_in,
        src_in,
        time_in,
        dst_in,
        dslot_in,
        asks,
        slots,
        gaps,
        freq_in,
        phase_in,
        w_input,
        b_input_in,
        w_hidden,
        b_hidden_in,
        w_query,
        w_key,
        w_value,
        w_merge,
        b_merge_in,
        w_out,
        b_out_in,
    ) = staged
    (
        hilo,
        ints,
        ibuf,
        req,
        reqr,
        gsend,
        grecv,
        ohg,
        ohs,
        oht,
        group,
        timed,
        touched,
        inverse,
        rows,
        store,
        answers,
        arrived,
        asked,
        ask_ones,
        ask_rest,
        slot_ones,
        slot_rest,
        picked,
        near_timed,
        scores,
        values,
        in_sem,
        ysend_sem,
        yrecv_sem,
        rsend_sem,
        rrecv_sem,
        gsend_sem,
        grecv_sem,
        up_send,
        up_recv,
        down_send,
        down_recv,
        ask_send,
        ask_recv,
        answer_send,
        answer_recv,
    ) = scratch[22:]

    me_t = lax.axis_index("tm")
    me = lax.axis_index("dom")
    nz = domains // GROUP
    my_z, my_j = me // GROUP, me % GROUP
    nodes, width = cur.shape
    half = nodes // 2
    neighbours, events = slots.shape
    er = events // 128
    asked_rows = domains * DCAP

    def fetch(i):
        return pltpu.make_async_copy(inputs[i], staged[i], in_sem.at[i])

    order = [4, 2, 3, 5, 6] + [0, 1] + list(range(7, 22))
    for i in order:
        fetch(i).start()

    barrier = pltpu.get_barrier_semaphore()

    def greet(i, carry):
        pl.semaphore_signal(
            barrier,
            inc=1,
            device_id={"dom": lax.rem(me + i, domains)},
            device_id_type=MESH,
        )
        return carry

    lax.fori_loop(1, domains, greet, 0)
    for i in range(1, periods):
        pl.semaphore_signal(
            barrier,
            inc=1,
            device_id={"tm": lax.rem(me_t + i, periods)},
            device_id_type=MESH,
        )
    for i in order[:5]:
        fetch(i).wait()
    row = 0
    ints[...] = jnp.zeros_like(ints)
    for ref in (dst_in, src_in, time_in, dslot_in):
        for j in range(ref.shape[1] // 128):
            ints[row : row + 1, :] = ref[:, j * 128 : (j + 1) * 128]
            row += 1
    ar = dst_in.shape[1] // 128
    pl.semaphore_wait(barrier, domains - 1 + periods - 1)

    for i in range(1, periods):
        start_copy(
            ints, ibuf.at[me_t], ysend_sem, yrecv_sem, {"tm": lax.rem(me_t + i, periods)}
        )

    mates = [(1, 0), (3, 0), (1, 1), (3, 1), (2, 0), (2, 1), (0, 1)]
    if GROUP == 2:
        mates = [(0, 1)]

    def mate(dx, dc):
        return ((my_j // 2 + dx) % (GROUP // 2)) * 2 + (my_j + dc) % 2

    for dx, dc in mates:
        peer = mate(dx, dc)
        start_copy(
            asks.at[:, peer], asked.at[my_j], ask_send, ask_recv, {"dom": my_z * GROUP + peer}
        )
    asked[my_j] = asks[:, my_j]
    for i in order[5:]:
        fetch(i).wait()
    hi, lo = split(cur[...])
    hilo[:, :width] = hi
    hilo[:, width:] = lo
    freq = freq_in[...].reshape(1, -1)
    phase = phase_in[...].reshape(1, -1)
    b_input = b_input_in[...].reshape(1, -1)
    b_hidden = b_hidden_in[...].reshape(1, -1)
    ibuf[me_t] = ints[...]
    others = ibuf.at[pl.ds(0, periods - 1)]
    wait_bytes(others, yrecv_sem)

    lanes = lax.broadcasted_iota(jnp.int32, (domains, 128), 1)
    subs = lax.broadcasted_iota(jnp.int32, (domains, 128), 0)
    mine = lanes // DCAP == subs % (128 // DCAP)
    tile = jnp.zeros((domains, 128), F32)
    fold_from = lax.broadcasted_iota(jnp.int32, (128, 128), 0)
    fold_to = lax.broadcasted_iota(jnp.int32, (128, 128), 1)
    for b in range(periods):
        wide = jnp.concatenate(
            [
                jnp.broadcast_to(ibuf[b, j : j + 1, :], (min(16, domains), 128))
                for j in range(max(ar, 1))
            ],
            axis=0,
        )
        kept = jnp.where(mine, wide, 0).astype(F32)
        top = jnp.floor(kept * (1 / 32))
        fold = jnp.where(
            (fold_to // DCAP == b) & (fold_from % DCAP == fold_to % DCAP), 1.0, 0.0
        ).astype(BF)
        tile = tile + 32.0 * dot(top.astype(BF), fold) + dot((kept - 32.0 * top).astype(BF), fold)
    req[...] = tile.astype(jnp.int32)[:, None, :]

    def peer_of(t):
        q, j = t % nz, t // nz
        odd = q % 2
        dz = odd * ((q + 1) // 2) + (1 - odd) * ((nz - q // 2) % nz)
        return ((my_z + dz) % nz) * GROUP + (my_j + j) % GROUP

    def ask(t, carry):
        peer = peer_of(t)
        start_copy(req.at[peer], reqr.at[me], rsend_sem, rrecv_sem, {"dom": peer})
        return carry

    lax.fori_loop(1, domains, ask, 0)
    reqr[me] = req[me]

    def prepare(b, stamps):
        at = b % 2
        source_rows = ibuf[b, pl.ds(ar, er), :]
        source = as_column(source_rows)
        moment = as_column(ibuf[b, pl.ds(ar + er, er), :])
        source_row = as_row(source_rows).astype(F32)
        nodes_lane = lax.broadcasted_iota(jnp.int32, (events, nodes), 1).astype(F32)
        picks = source == nodes_lane
        ohs[at] = jnp.where(picks, 1.0, 0.0).astype(BF)
        before = jnp.sum(jnp.where(picks, stamps, 0.0), axis=1, keepdims=True)
        latest = jnp.max(jnp.where(picks, moment, -1.0), axis=0, keepdims=True)
        same = source == source_row
        same_f = jnp.where(same, 1.0, 0.0)
        group[at] = same_f.astype(BF)
        inverse[at] = jnp.broadcast_to(
            1.0 / jnp.sum(same_f, axis=1, keepdims=True), inverse.shape[1:]
        )
        earlier = lax.broadcasted_iota(jnp.int32, same.shape, 0) < lax.broadcasted_iota(
            jnp.int32, same.shape, 1
        )
        first = jnp.sum(jnp.where(same & earlier, 1.0, 0.0), axis=0, keepdims=True) == 0.0
        nodes_sub = lax.broadcasted_iota(jnp.int32, (nodes, events), 0).astype(F32)
        back = jnp.where((source_row == nodes_sub) & first, 1.0, 0.0)
        oht[at] = back.astype(BF)
        touched[at] = jnp.broadcast_to(jnp.sum(back, axis=1, keepdims=True), touched.shape[1:])
        code = cosine((moment - before) * freq + phase).astype(BF)
        timed[at] = dot(code, w_input[2 * width :, :])
        return jnp.where(latest >= 0.0, latest, stamps)

    def asked_picks(b):
        wide = jnp.broadcast_to(reqr[...], (domains, DCAP, 128)).reshape(asked_rows, 128)
        lanes = lax.broadcasted_iota(jnp.int32, (asked_rows, 128), 1)
        subs = lax.broadcasted_iota(jnp.int32, (asked_rows, 128), 0)
        wanted = jnp.sum(
            jnp.where(lanes == b * DCAP + subs % DCAP, wide.astype(F32), 0.0),
            axis=1,
            keepdims=True,
        )
        ones, rest = two_level(wanted)
        ohg[b % 2] = picks_of(ones, rest, jnp.bfloat16(0), nodes // 128)

    def near_prepare(k, carry):
        here = pl.ds(k * events, events)
        gap, slot = [
            jnp.concatenate(
                [
                    as_column(ref[pl.ds(k, 1), :][:, j * 128 : (j + 1) * 128])
                    for j in range(events // 128)
                ],
                axis=0,
            )
            for ref in (gaps, slots)
        ]
        code = cosine(gap * freq + phase).astype(BF)
        near_timed[here, :width] = dot(code, w_key[width:, :])
        near_timed[here, width:] = dot(code, w_value[width:, :])
        ones, rest = two_level(slot)
        slot_ones[here, :] = ones
        slot_rest[here, :] = rest
        return carry

    def ask_prepare(z, carry):
        for j in range(GROUP):
            ones, rest = two_level(as_column(asked[j, z]))
            ask_ones[z, j * CAP : (j + 1) * CAP, :] = ones
            ask_rest[z, j * CAP : (j + 1) * CAP, :] = rest
        return carry

    def give(b):
        answer = dot(ohg[b % 2], hilo[:, :width])
        gsend[b] = jnp.concatenate(
            [
                answer[:, :128].reshape(domains, DCAP, 128),
                answer[:, 128:].reshape(domains, DCAP, 128),
            ],
            axis=1,
        ).astype(BF)

        def send(t, carry):
            peer = peer_of(t)
            start_copy(
                gsend.at[b, peer],
                grecv.at[b, me],
                gsend_sem.at[b],
                grecv_sem.at[b],
                {"dom": peer},
            )
            return carry

        lax.fori_loop(1, domains, send, 0)
        grecv[b, me] = gsend[b, me]

    def own_share(b):
        own = dot(ohs[b % 2], hilo[...])
        own_hi = own[:, :width].astype(BF)
        own_f = own[:, :width] + own[:, width:]
        projected = dot(own_hi, w_input[:width, :]) + timed[b % 2]
        hidden = dot(own_hi, w_hidden[...]) + b_hidden
        slot = as_column(ibuf[b, pl.ds(ar + 2 * er, er), :]).astype(jnp.int32)
        place = (slot // DCAP) * (2 * DCAP) + slot % DCAP
        lane = lax.broadcasted_iota(jnp.int32, (events, 2 * asked_rows), 1)
        pick_left = jnp.where(lane == place, 1.0, 0.0).astype(BF)
        pick_right = jnp.where(lane == place + DCAP, 1.0, 0.0).astype(BF)
        return own_f, projected, hidden, pick_left, pick_right

    def update(b, share):
        own_f, projected, hidden, pick_left, pick_right = share
        wait_bytes(grecv.at[b, pl.ds(0, domains - 1)], grecv_sem.at[b])
        fetched = grecv[b].reshape(2 * asked_rows, 128)
        target = jnp.concatenate(
            [dot(pick_left, fetched), dot(pick_right, fetched)], axis=1
        ).astype(BF)
        projected = projected + dot(target, w_input[width : 2 * width, :])
        p_hi, p_lo = split(projected)
        at = b % 2
        gates = (dot(group[at], p_hi) + dot(group[at], p_lo)) * inverse[at][:, :1] + b_input
        r = jax.nn.sigmoid(gates[:, :width] + hidden[:, :width])
        z = jax.nn.sigmoid(gates[:, width : 2 * width] + hidden[:, width : 2 * width])
        c = jnp.tanh(gates[:, 2 * width :] + r * hidden[:, 2 * width :])
        fresh = (1.0 - z) * c + z * own_f
        f_hi, f_lo = split(fresh)
        spread = dot(oht[at], jnp.concatenate([f_hi, f_lo], axis=1))
        updated = jnp.where(
            touched[at][:, :1] > 0.0, spread[:, :width] + spread[:, width:], cur[...]
        )

        @pl.when(me_t == b)
        def _():
            out_memory[...] = updated

        if b + 1 < periods:
            cur[...] = updated
            hilo[:, :width] = updated.astype(BF)

    stamps = prepare(0, stamps_in[...].reshape(1, -1).astype(F32))
    wait_bytes(reqr.at[pl.ds(0, domains - 1)], rrecv_sem)
    asked_picks(0)

    def spans(count, parts):
        edges = [count * i // parts for i in range(parts + 1)]
        return list(zip(edges[:-1], edges[1:]))

    beside_near = spans(neighbours, periods - 1)
    beside_asks = spans(nz, periods - 1)
    for b in range(periods - 1):
        give(b)
        if b:
            hilo[:, width:] = (cur[...] - hilo[:, :width].astype(F32)).astype(BF)

        @pl.when(me_t == b)
        def _():
            rows[...] = hilo[:, :width]

        share = own_share(b)
        asked_picks(b + 1)
        stamps = prepare(b + 1, stamps)
        lax.fori_loop(*beside_near[b], near_prepare, 0)
        if b == 0:
            wait_bytes(asked.at[pl.ds(0, GROUP - 1)], ask_recv)
        lax.fori_loop(*beside_asks[b], ask_prepare, 0)
        update(b, share)

    @pl.when(me_t == periods - 1)
    def _():
        rows[...] = hilo[:, :width]

    offsets = [0]
    for step in range(1, nz // 2):
        offsets += [step, -step]
    offsets += [nz // 2]
    above = lax.rem(me + GROUP, domains)
    below = lax.rem(me + domains - GROUP, domains)
    last = nz // 2 - 1

    def pass_on(step, part, up):
        origin = lax.rem(my_z + (nz - step if up else step), nz)
        span = pl.ds(part * half, half)
        src = rows.at[span] if step == 0 else store.at[origin, span]
        send, recv = (up_send, up_recv) if up else (down_send, down_recv)
        return pltpu.make_async_remote_copy(
            src_ref=src,
            dst_ref=store.at[origin, span],
            send_sem=send.at[step, part],
            recv_sem=recv.at[step, part],
            device_id={"dom": above if up else below},
            device_id_type=MESH,
        )

    def take(step, part, up):
        origin = lax.rem(my_z + (nz - step - 1 if up else step + 1), nz)
        recv = up_recv if up else down_recv
        wait_bytes(store.at[origin, pl.ds(part * half, half)], recv.at[step, part])

    def moves(step, part, up):
        return step < last or part == (0 if up else 1)

    def answer(i):
        offset = offsets[i]
        origin = lax.rem(my_z + offset + nz, nz)
        if offset:
            step = abs(offset) - 1
            for part in range(2):
                up = offset < 0 if step < last else part == 0
                take(step, part, up)
                if step < last and moves(step + 1, part, up):
                    pass_on(step + 1, part, up).start()
        block = rows if offset == 0 else store.at[origin]
        size = GROUP * CAP // HALVES
        for side in range(HALVES):
            here = pl.ds(side * size, size)
            pick = picks_of(
                ask_ones[origin, here, :],
                ask_rest[origin, here, :],
                jnp.bfloat16(0),
                nodes // 128,
            )
            found = dot(pick, block[...]).astype(BF)
            answers[i, pl.ds(side * (GROUP // HALVES), GROUP // HALVES)] = found.reshape(
                GROUP // HALVES, CAP, width
            )
        for dx, dc in mates:
            peer = mate(dx, dc)
            start_copy(
                answers.at[i, peer],
                arrived.at[i, my_j],
                answer_send.at[i],
                answer_recv.at[i],
                {"dom": my_z * GROUP + peer},
            )
        arrived[i, my_j] = answers[i, my_j]

    def select(i):
        origin = lax.rem(my_z + offsets[i] + nz, nz)
        wait_bytes(arrived.at[i, pl.ds(0, GROUP - 1)], answer_recv.at[i])
        first = jnp.full((1, 128), origin * GROUP, jnp.int32).astype(F32).astype(BF)

        def some(k, carry):
            here = pl.ds(k * 2 * events, 2 * events)
            pick = picks_of(slot_ones[here, :], slot_rest[here, :], first, GROUP)
            part = dot(pick, arrived[i].reshape(GROUP * CAP, width)).astype(BF)
            if i == 0:
                picked[here, :] = part
            else:
                picked[here, :] = picked[here, :] + part
            return carry

        lax.fori_loop(0, neighbours // 2, some, 0)

    for part in range(2):
        for up in (True, False):
            if moves(0, part, up):
                pass_on(0, part, up).start()
    answer(0)
    final = periods - 1
    give(final)
    hilo[:, width:] = (cur[...] - hilo[:, :width].astype(F32)).astype(BF)

    src_col = as_column(ints[pl.ds(ar, er), :])
    lane = lax.broadcasted_iota(jnp.int32, (events, nodes), 1).astype(F32)
    own = dot(jnp.where(src_col == lane, 1.0, 0.0).astype(BF), rows[...]).astype(BF)
    still = jnp.broadcast_to(cosine(phase).astype(BF), (events, width))
    query = (dot(own, w_query[:width, :]) + dot(still, w_query[width:, :])).astype(BF)

    for i in range(1, nz):
        answer(i)
        if i == 2:
            update(final, own_share(final))
        select(i - 1)
    select(nz - 1)

    head = width // HEADS
    same_head = (
        lax.broadcasted_iota(jnp.int32, (width, width), 0) // head
        == lax.broadcasted_iota(jnp.int32, (width, width), 1) // head
    )
    heads = jnp.where(same_head, 1.0, 0.0).astype(BF)
    query_f = query.astype(F32)
    query_2 = jnp.concatenate([query_f, query_f], axis=0)

    def score(k, carry):
        here = pl.ds(k * 2 * events, 2 * events)
        near = picked[here, :]
        key = (dot(near, w_key[:width, :]) + near_timed[here, :width]).astype(BF)
        values[here, :] = (dot(near, w_value[:width, :]) + near_timed[here, width:]).astype(BF)
        hi, lo = split(query_2 * key.astype(F32))
        scores[here, :] = (dot(hi, heads) + dot(lo, heads)) * (1.0 / math.sqrt(head))
        return carry

    lax.fori_loop(0, neighbours // 2, score, 0)

    def slab(ref, k):
        return ref[k * events : (k + 1) * events, :]

    top = slab(scores, 0)
    for k in range(1, neighbours):
        top = jnp.maximum(top, slab(scores, k))
    total = jnp.zeros_like(top)
    for k in range(neighbours):
        raised = jnp.exp(slab(scores, k) - top)
        scores[k * events : (k + 1) * events, :] = raised
        total = total + raised
    scale = 1.0 / total
    attended = jnp.zeros_like(top)
    for k in range(neighbours):
        weight = (slab(scores, k) * scale).astype(BF).astype(F32)
        attended = attended + weight * slab(values, k).astype(F32)
    merged = dot(attended.astype(BF), w_merge[:width, :]) + dot(own, w_merge[width:, :])
    merged = jnp.maximum(merged + b_merge_in[...].reshape(1, -1), 0.0).astype(BF)
    out[...] = (dot(merged, w_out[...]) + b_out_in[...].reshape(1, -1)).astype(BF)

    wait_bytes(others, ysend_sem)
    wait_bytes(reqr.at[pl.ds(0, domains - 1)], rsend_sem)
    for b in range(periods):
        wait_bytes(gsend.at[b, pl.ds(0, domains - 1)], gsend_sem.at[b])
    for step in range(nz // 2):
        for part in range(2):
            for up in (True, False):
                if moves(step, part, up):
                    pass_on(step, part, up).wait_send()
    wait_bytes(asked.at[pl.ds(0, GROUP - 1)], ask_send)
    for i in range(nz):
        wait_bytes(answers.at[i, pl.ds(0, GROUP - 1)], answer_send.at[i])


def on_device(*args):
    periods, domains = lax.axis_size("tm"), lax.axis_size("dom")
    nz = domains // GROUP
    nodes, width = args[0].shape
    neighbours, events = args[7].shape[1:]
    pairs = neighbours * events
    asked = domains * DCAP
    inputs = list(args)
    inputs[6] = args[6].reshape(nz, GROUP, 1, CAP)
    inputs[7] = args[7][0]
    inputs[8] = args[8][0]
    staged = [pltpu.VMEM(a.shape, a.dtype) for a in inputs]
    dma = pltpu.SemaphoreType.DMA
    updated, embedded = pl.pallas_call(
        functools.partial(whole_kernel, periods, domains),
        out_shape=(
            jax.ShapeDtypeStruct((nodes, width), F32),
            jax.ShapeDtypeStruct((events, width), BF),
        ),
        in_specs=[pl.BlockSpec(memory_space=pl.ANY)] * len(inputs),
        out_specs=[pl.BlockSpec(memory_space=pltpu.VMEM)] * 2,
        scratch_shapes=staged
        + [
            pltpu.VMEM((nodes, 2 * width), BF),
            pltpu.VMEM((16, 128), jnp.int32),
            pltpu.VMEM((periods, 16, 128), jnp.int32),
            pltpu.VMEM((domains, 1, 128), jnp.int32),
            pltpu.VMEM((domains, 1, 128), jnp.int32),
            pltpu.VMEM((periods, domains, 2 * DCAP, 128), BF),
            pltpu.VMEM((periods, domains, 2 * DCAP, 128), BF),
            pltpu.VMEM((2, asked, nodes), BF),
            pltpu.VMEM((2, events, nodes), BF),
            pltpu.VMEM((2, nodes, events), BF),
            pltpu.VMEM((2, events, events), BF),
            pltpu.VMEM((2, events, 3 * width), F32),
            pltpu.VMEM((2, nodes, 128), F32),
            pltpu.VMEM((2, events, 128), F32),
            pltpu.VMEM((nodes, width), BF),
            pltpu.VMEM((nz, nodes, width), BF),
            pltpu.VMEM((nz, GROUP, CAP, width), BF),
            pltpu.VMEM((nz, GROUP, CAP, width), BF),
            pltpu.VMEM((GROUP, nz, 1, CAP), jnp.int32),
            pltpu.VMEM((nz, GROUP * CAP, 128), BF),
            pltpu.VMEM((nz, GROUP * CAP, 128), BF),
            pltpu.VMEM((pairs, 128), BF),
            pltpu.VMEM((pairs, 128), BF),
            pltpu.VMEM((pairs, width), BF),
            pltpu.VMEM((pairs, 2 * width), F32),
            pltpu.VMEM((pairs, width), F32),
            pltpu.VMEM((pairs, width), BF),
            dma((len(inputs),)),
            dma(()),
            dma(()),
            dma(()),
            dma(()),
            dma((periods,)),
            dma((periods,)),
            dma((nz // 2, 2)),
            dma((nz // 2, 2)),
            dma((nz // 2, 2)),
            dma((nz // 2, 2)),
            dma(()),
            dma(()),
            dma((nz,)),
            dma((nz,)),
        ],
        compiler_params=pltpu.CompilerParams(
            collective_id=0, has_side_effects=True, vmem_limit_bytes=60 * 2**20
        ),
        name="whole",
    )(*inputs)
    return (updated[None], embedded[None])


def solution(mesh):
    return jax.shard_map(
        on_device,
        mesh=mesh,
        in_specs=(
            P("dom", None),
            P("dom"),
            P("tm", "dom"),
            P("tm", "dom"),
            P("tm", "dom"),
            P("tm", "dom"),
            P("tm", "dom"),
            P("tm", None, "dom"),
            P("tm", None, "dom"),
            P(),
            P(),
            P(),
            P(),
            P(),
            P(),
            P(),
            P(),
            P(),
            P(),
            P(),
            P(),
            P(),
        ),
        out_specs=(P("tm", "dom", None), P("tm", "dom", None)),
        check_vma=False,
    )
```

```python
import functools
import math

import jax
import jax.numpy as jnp
from jax import lax
from jax.experimental import pallas as pl
from jax.experimental.pallas import tpu as pltpu
from jax.sharding import PartitionSpec as P

HEADS = 4
GROUP = 8
DCAP = 8
CAP = 128
HALVES = 2
LATE = 3
MESH = pl.DeviceIdType.MESH
BF = jnp.bfloat16
F32 = jnp.float32


def cosine(x):
    turns = jnp.floor(x * (0.5 / math.pi) + 0.5)
    h = 0.5 * ((x - turns * 6.28125) - turns * (2 * math.pi - 6.28125))
    q = h * h
    s = h + h * q * (
        -1 / 6 + q * (1 / 120 + q * (-1 / 5040 + q * (1 / 362880 - q * (1 / 39916800))))
    )
    return 1.0 - 2.0 * s * s


def dot(a, b):
    return jnp.dot(a, b, preferred_element_type=F32)


def as_column(row):
    lanes = lax.broadcasted_iota(jnp.int32, (128, 128), 1)
    subs = lax.broadcasted_iota(jnp.int32, (128, 128), 0)
    parts = []
    for i in range(row.shape[0]):
        wide = jnp.broadcast_to(row[i : i + 1, :].astype(F32), (128, 128))
        parts.append(jnp.sum(jnp.where(lanes == subs, wide, 0.0), axis=1, keepdims=True))
    return jnp.concatenate(parts, axis=0)


def as_row(row):
    return jnp.concatenate([row[i : i + 1, :] for i in range(row.shape[0])], axis=1)


def split(x):
    hi = x.astype(BF)
    return hi, (x - hi.astype(F32)).astype(BF)


def two_level(column):
    rest = jnp.floor(column * (1 / 128))
    lanes = lax.broadcasted_iota(jnp.int32, (column.shape[0], 128), 1).astype(F32)
    ones = jnp.where(column - rest * 128 == lanes, 1.0, 0.0).astype(BF)
    return ones, jnp.broadcast_to(rest, ones.shape).astype(BF)


def picks_of(ones, rest, first, count):
    none = jnp.zeros_like(ones)
    return jnp.concatenate(
        [jnp.where(rest == first + jnp.bfloat16(t), ones, none) for t in range(count)], axis=1
    )


def start_copy(src, dst, send_sem, recv_sem, device_id):
    copy = pltpu.make_async_remote_copy(
        src_ref=src,
        dst_ref=dst,
        send_sem=send_sem,
        recv_sem=recv_sem,
        device_id=device_id,
        device_id_type=MESH,
    )
    copy.start()


def wait_bytes(ref, sem):
    pltpu.make_async_copy(ref, ref, sem).wait()


def whole_kernel(periods, domains, *refs):
    inputs, (out_memory, out), scratch = refs[:22], refs[22:24], refs[24:]
    staged = scratch[:22]
    (
        cur,
        stamps_in,
        src_in,
        time_in,
        dst_in,
        dslot_in,
        asks_in,
        slots,
        gaps,
        freq_in,
        phase_in,
        w_input,
        b_input_in,
        w_hidden,
        b_hidden_in,
        w_query,
        w_key,
        w_value,
        w_merge,
        b_merge_in,
        w_out,
        b_out_in,
    ) = staged
    (
        fresh_memory,
        asks,
        hilo,
        ints,
        ibuf,
        req,
        reqr,
        gsend,
        grecv,
        ohg,
        ohs,
        oht,
        group,
        timed,
        touched,
        inverse,
        rows,
        store,
        answers,
        arrived,
        asked,
        ask_ones,
        ask_rest,
        slot_ones,
        slot_rest,
        picked,
        near_timed,
        scores,
        values,
        in_sem,
        out_sem,
        ysend_sem,
        yrecv_sem,
        rsend_sem,
        rrecv_sem,
        gsend_sem,
        grecv_sem,
        up_send,
        up_recv,
        down_send,
        down_recv,
        ask_send,
        ask_recv,
        answer_send,
        answer_recv,
    ) = scratch[22:]

    me_t = lax.axis_index("tm")
    me = lax.axis_index("dom")
    nz = domains // GROUP
    my_z, my_j = me // GROUP, me % GROUP
    nodes, width = cur.shape
    half = nodes // 2
    neighbours, events = slots.shape
    er = events // 128
    asked_rows = domains * DCAP

    def fetch(i):
        return pltpu.make_async_copy(inputs[i], staged[i], in_sem.at[i])

    order = [4, 2, 3, 5, 6] + [0, 1] + list(range(7, 22))
    for i in order:
        fetch(i).start()

    barrier = pltpu.get_barrier_semaphore()

    ways = [nz // 2] + [w for step in range(nz // 2 - 1, 0, -1) for w in (step, nz - step)] + [0]
    bases = [lax.rem(my_z + way, nz) * GROUP for way in ways]

    def each_peer(visit):
        for base in bases[:-1]:
            visit(base + my_j)

        def some(j, carry):
            place = lax.rem(my_j + j, GROUP)
            for base in bases:
                visit(base + place)
            return carry

        lax.fori_loop(1, GROUP, some, 0)

    def greet(peer):
        pl.semaphore_signal(
            barrier, inc=1, device_id={"dom": peer}, device_id_type=MESH
        )

    each_peer(greet)
    for i in range(1, periods):
        pl.semaphore_signal(
            barrier,
            inc=1,
            device_id={"tm": lax.rem(me_t + i, periods)},
            device_id_type=MESH,
        )
    for i in order[:5]:
        fetch(i).wait()
    row = 0
    ints[...] = jnp.zeros_like(ints)
    for ref in (dst_in, src_in, time_in, dslot_in):
        for j in range(ref.shape[1] // 128):
            ints[row : row + 1, :] = ref[:, j * 128 : (j + 1) * 128]
            row += 1
    ar = dst_in.shape[1] // 128
    for z in range(nz):
        for j in range(GROUP):
            at = (z * GROUP + j) * CAP
            asks[z, j] = asks_in[:, at : at + CAP]
    pl.semaphore_wait(barrier, domains - 1 + periods - 1)

    for i in range(1, periods):
        start_copy(
            ints, ibuf.at[me_t], ysend_sem, yrecv_sem, {"tm": lax.rem(me_t + i, periods)}
        )

    mates = [(1, 0), (3, 0), (1, 1), (3, 1), (2, 0), (2, 1), (0, 1)]
    if GROUP == 2:
        mates = [(0, 1)]

    def mate(dx, dc):
        return ((my_j // 2 + dx) % (GROUP // 2)) * 2 + (my_j + dc) % 2

    for dx, dc in mates:
        peer = mate(dx, dc)
        start_copy(
            asks.at[:, peer], asked.at[my_j], ask_send, ask_recv, {"dom": my_z * GROUP + peer}
        )
    asked[my_j] = asks[:, my_j]
    for i in order[5:]:
        fetch(i).wait()
    hi, lo = split(cur[...])
    hilo[:, :width] = hi
    hilo[:, width:] = lo
    freq = freq_in[...].reshape(1, -1)
    phase = phase_in[...].reshape(1, -1)
    b_input = b_input_in[...].reshape(1, -1)
    b_hidden = b_hidden_in[...].reshape(1, -1)
    ibuf[me_t] = ints[...]

    def near_prepare(k, carry):
        here = pl.ds(k * events, events)
        gap, slot = [
            jnp.concatenate(
                [
                    as_column(ref[pl.ds(k, 1), :][:, j * 128 : (j + 1) * 128])
                    for j in range(events // 128)
                ],
                axis=0,
            )
            for ref in (gaps, slots)
        ]
        code = cosine(gap * freq + phase).astype(BF)
        near_timed[here, :width] = dot(code, w_key[width:, :])
        near_timed[here, width:] = dot(code, w_value[width:, :])
        ones, rest = two_level(slot)
        slot_ones[here, :] = ones
        slot_rest[here, :] = rest
        return carry

    lax.fori_loop(0, 2, near_prepare, 0)
    others = ibuf.at[pl.ds(0, periods - 1)]
    wait_bytes(others, yrecv_sem)

    lanes = lax.broadcasted_iota(jnp.int32, (domains, 128), 1)
    subs = lax.broadcasted_iota(jnp.int32, (domains, 128), 0)
    mine = lanes // DCAP == subs % (128 // DCAP)
    tile = jnp.zeros((domains, 128), F32)
    fold_from = lax.broadcasted_iota(jnp.int32, (128, 128), 0)
    fold_to = lax.broadcasted_iota(jnp.int32, (128, 128), 1)
    for b in range(periods):
        wide = jnp.concatenate(
            [
                jnp.broadcast_to(ibuf[b, j : j + 1, :], (min(16, domains), 128))
                for j in range(max(ar, 1))
            ],
            axis=0,
        )
        kept = jnp.where(mine, wide, 0).astype(F32)
        top = jnp.floor(kept * (1 / 32))
        fold = jnp.where(
            (fold_to // DCAP == b) & (fold_from % DCAP == fold_to % DCAP), 1.0, 0.0
        ).astype(BF)
        tile = tile + 32.0 * dot(top.astype(BF), fold) + dot((kept - 32.0 * top).astype(BF), fold)
    req[...] = tile.astype(jnp.int32)[:, None, :]

    def ask(peer):
        start_copy(req.at[peer], reqr.at[me], rsend_sem, rrecv_sem, {"dom": peer})

    each_peer(ask)
    reqr[me] = req[me]

    def prepare(b, stamps):
        at = b % 2
        source_rows = ibuf[b, pl.ds(ar, er), :]
        source = as_column(source_rows)
        moment = as_column(ibuf[b, pl.ds(ar + er, er), :])
        source_row = as_row(source_rows).astype(F32)
        nodes_lane = lax.broadcasted_iota(jnp.int32, (events, nodes), 1).astype(F32)
        picks = source == nodes_lane
        ohs[at] = jnp.where(picks, 1.0, 0.0).astype(BF)
        before = jnp.sum(jnp.where(picks, stamps, 0.0), axis=1, keepdims=True)
        latest = jnp.max(jnp.where(picks, moment, -1.0), axis=0, keepdims=True)
        same = source == source_row
        same_f = jnp.where(same, 1.0, 0.0)
        group[at] = same_f.astype(BF)
        inverse[at] = jnp.broadcast_to(
            1.0 / jnp.sum(same_f, axis=1, keepdims=True), inverse.shape[1:]
        )
        earlier = lax.broadcasted_iota(jnp.int32, same.shape, 0) < lax.broadcasted_iota(
            jnp.int32, same.shape, 1
        )
        first = jnp.sum(jnp.where(same & earlier, 1.0, 0.0), axis=0, keepdims=True) == 0.0
        nodes_sub = lax.broadcasted_iota(jnp.int32, (nodes, events), 0).astype(F32)
        back = jnp.where((source_row == nodes_sub) & first, 1.0, 0.0)
        oht[at] = back.astype(BF)
        touched[at] = jnp.broadcast_to(jnp.sum(back, axis=1, keepdims=True), touched.shape[1:])
        code = cosine((moment - before) * freq + phase).astype(BF)
        timed[at] = dot(code, w_input[2 * width :, :])
        return jnp.where(latest >= 0.0, latest, stamps)

    def asked_picks(b):
        wide = jnp.broadcast_to(reqr[...], (domains, DCAP, 128)).reshape(asked_rows, 128)
        lanes = lax.broadcasted_iota(jnp.int32, (asked_rows, 128), 1)
        subs = lax.broadcasted_iota(jnp.int32, (asked_rows, 128), 0)
        wanted = jnp.sum(
            jnp.where(lanes == b * DCAP + subs % DCAP, wide.astype(F32), 0.0),
            axis=1,
            keepdims=True,
        )
        ones, rest = two_level(wanted)
        ohg[b % 2] = picks_of(ones, rest, jnp.bfloat16(0), nodes // 128)

    def ask_prepare(z):
        for j in range(GROUP):
            ones, rest = two_level(as_column(asked[j, z]))
            ask_ones[z, j * CAP : (j + 1) * CAP, :] = ones
            ask_rest[z, j * CAP : (j + 1) * CAP, :] = rest

    def put_answer(b, answer):
        gsend[b] = jnp.concatenate(
            [
                answer[:, :128].reshape(domains, DCAP, 128),
                answer[:, 128:].reshape(domains, DCAP, 128),
            ],
            axis=1,
        ).astype(BF)

    def give(b):
        def send(peer):
            start_copy(
                gsend.at[b, peer],
                grecv.at[b, me],
                gsend_sem.at[b],
                grecv_sem.at[b],
                {"dom": peer},
            )

        each_peer(send)
        grecv[b, me] = gsend[b, me]

    def own_share(b):
        at = b % 2
        own = dot(ohs[at], hilo[...])
        own_hi = own[:, :width].astype(BF)
        own_f = own[:, :width] + own[:, width:]
        p_hi, p_lo = split(dot(own_hi, w_input[:width, :]) + timed[at])
        base = (dot(group[at], p_hi) + dot(group[at], p_lo)) * inverse[at][:, :1] + b_input
        hidden = dot(own_hi, w_hidden[...]) + b_hidden
        slot = as_column(ibuf[b, pl.ds(ar + 2 * er, er), :]).astype(jnp.int32)
        place = (slot // DCAP) * (2 * DCAP) + slot % DCAP
        lane = lax.broadcasted_iota(jnp.int32, (events, 2 * asked_rows), 1)
        sums = [
            dot(group[at], jnp.where(lane == place + j * DCAP, 1.0, 0.0).astype(BF)).astype(BF)
            for j in range(2)
        ]
        return own_f, base, hidden, sums

    def next_share(b):
        through = dot(ohg[b % 2], oht[(b - 1) % 2])
        kept = jnp.where(
            jnp.sum(through, axis=1, keepdims=True) > 0.0, 0.0, dot(ohg[b % 2], hilo[:, :width])
        )
        return through.astype(BF), kept

    def update(b, share):
        own_f, base, hidden, sums = share
        wait_bytes(grecv.at[b, pl.ds(0, domains - 1)], grecv_sem.at[b])
        fetched = grecv[b].reshape(2 * asked_rows, 128)
        total = jnp.concatenate([dot(sums[0], fetched), dot(sums[1], fetched)], axis=1)
        m_hi, m_lo = split(total * inverse[b % 2][:, :1])
        w_target = w_input[width : 2 * width, :]
        gates = base + dot(m_hi, w_target) + dot(m_lo, w_target)
        r = jax.nn.sigmoid(gates[:, :width] + hidden[:, :width])
        z = jax.nn.sigmoid(gates[:, width : 2 * width] + hidden[:, width : 2 * width])
        c = jnp.tanh(gates[:, 2 * width :] + r * hidden[:, 2 * width :])
        return split((1.0 - z) * c + z * own_f)

    def write_back(b, fresh):
        at = b % 2
        spread = dot(oht[at], jnp.concatenate(fresh, axis=1))
        updated = jnp.where(
            touched[at][:, :1] > 0.0, spread[:, :width] + spread[:, width:], cur[...]
        )

        @pl.when(me_t == b)
        def _():
            fresh_memory[...] = updated

        if b + 1 < periods:
            cur[...] = updated
            hi, lo = split(updated)
            hilo[:, :width] = hi
            hilo[:, width:] = lo

    stamps = prepare(0, stamps_in[...].reshape(1, -1).astype(F32))
    lax.fori_loop(2, 4, near_prepare, 0)
    wait_bytes(reqr.at[pl.ds(0, domains - 1)], rrecv_sem)
    asked_picks(0)

    put_answer(0, dot(ohg[0], hilo[:, :width]))
    for b in range(periods - 1):
        give(b)
        if b:
            write_back(b - 1, fresh)

        @pl.when(me_t == b)
        def _():
            rows[...] = hilo[:, :width]

        share = own_share(b)
        asked_picks(b + 1)
        stamps = prepare(b + 1, stamps)
        through, kept = next_share(b + 1)
        if b == 0:
            wait_bytes(asked.at[pl.ds(0, GROUP - 1)], ask_recv)
            ask_prepare(my_z)
        fresh = update(b, share)
        if b + 2 < periods:
            put_answer(b + 1, kept + dot(through, fresh[0]))
    write_back(periods - 2, fresh)

    @pl.when(me_t == periods - 1)
    def _():
        rows[...] = hilo[:, :width]

    offsets = [0]
    for step in range(1, nz // 2):
        offsets += [step, -step]
    offsets += [nz // 2]
    above = lax.rem(me + GROUP, domains)
    below = lax.rem(me + domains - GROUP, domains)
    last = nz // 2 - 1

    def pass_on(step, part, up):
        origin = lax.rem(my_z + (nz - step if up else step), nz)
        span = pl.ds(part * half, half)
        src = rows.at[span] if step == 0 else store.at[origin, span]
        send, recv = (up_send, up_recv) if up else (down_send, down_recv)
        return pltpu.make_async_remote_copy(
            src_ref=src,
            dst_ref=store.at[origin, span],
            send_sem=send.at[step, part],
            recv_sem=recv.at[step, part],
            device_id={"dom": above if up else below},
            device_id_type=MESH,
        )

    def take(step, part, up):
        origin = lax.rem(my_z + (nz - step - 1 if up else step + 1), nz)
        recv = up_recv if up else down_recv
        wait_bytes(store.at[origin, pl.ds(part * half, half)], recv.at[step, part])

    def moves(step, part, up):
        return step < last or part == (0 if up else 1)

    def answer(i):
        offset = offsets[i]
        origin = lax.rem(my_z + offset + nz, nz)
        if offset:
            step = abs(offset) - 1
            for part in range(2):
                up = offset < 0 if step < last else part == 0
                take(step, part, up)
                if step < last and moves(step + 1, part, up):
                    pass_on(step + 1, part, up).start()
        block = rows if offset == 0 else store.at[origin]
        size = GROUP * CAP // HALVES
        for side in range(HALVES):
            here = pl.ds(side * size, size)
            pick = picks_of(
                ask_ones[origin, here, :],
                ask_rest[origin, here, :],
                jnp.bfloat16(0),
                nodes // 128,
            )
            found = dot(pick, block[...]).astype(BF)
            answers[i, pl.ds(side * (GROUP // HALVES), GROUP // HALVES)] = found.reshape(
                GROUP // HALVES, CAP, width
            )
        for dx, dc in mates:
            peer = mate(dx, dc)
            start_copy(
                answers.at[i, peer],
                arrived.at[i, my_j],
                answer_send.at[i],
                answer_recv.at[i],
                {"dom": my_z * GROUP + peer},
            )
        arrived[i, my_j] = answers[i, my_j]

    def select(i):
        origin = lax.rem(my_z + offsets[i] + nz, nz)
        wait_bytes(arrived.at[i, pl.ds(0, GROUP - 1)], answer_recv.at[i])
        first = jnp.full((1, 128), origin * GROUP, jnp.int32).astype(F32).astype(BF)

        def some(k, carry):
            here = pl.ds(k * 2 * events, 2 * events)
            pick = picks_of(slot_ones[here, :], slot_rest[here, :], first, GROUP)
            part = dot(pick, arrived[i].reshape(GROUP * CAP, width)).astype(BF)
            if i == 0:
                picked[here, :] = part
            else:
                picked[here, :] = picked[here, :] + part
            return carry

        lax.fori_loop(0, neighbours // 2, some, 0)

    for part in range(2):
        for up in (True, False):
            if moves(0, part, up):
                pass_on(0, part, up).start()
    answer(0)
    final = periods - 1
    put_answer(final, kept + dot(through, fresh[0]))
    give(final)
    ask_prepare(lax.rem(my_z + offsets[1] + nz, nz))
    lax.fori_loop(4, neighbours, near_prepare, 0)

    src_col = as_column(ints[pl.ds(ar, er), :])
    lane = lax.broadcasted_iota(jnp.int32, (events, nodes), 1).astype(F32)
    own = dot(jnp.where(src_col == lane, 1.0, 0.0).astype(BF), rows[...]).astype(BF)
    still = jnp.broadcast_to(cosine(phase).astype(BF), (events, width))
    query = (dot(own, w_query[:width, :]) + dot(still, w_query[width:, :])).astype(BF)

    result = pltpu.make_async_copy(fresh_memory, out_memory, out_sem)
    for i in range(1, nz):
        answer(i)
        if i + 1 < nz:
            ask_prepare(lax.rem(my_z + offsets[i + 1] + nz, nz))
        select(i - 1)
        if i == LATE:
            write_back(final, update(final, own_share(final)))
            result.start()
    select(nz - 1)

    head = width // HEADS
    same_head = (
        lax.broadcasted_iota(jnp.int32, (width, width), 0) // head
        == lax.broadcasted_iota(jnp.int32, (width, width), 1) // head
    )
    heads = jnp.where(same_head, 1.0, 0.0).astype(BF)
    query_f = query.astype(F32)
    query_2 = jnp.concatenate([query_f, query_f], axis=0)

    def score(k, carry):
        here = pl.ds(k * 2 * events, 2 * events)
        near = picked[here, :]
        key = (dot(near, w_key[:width, :]) + near_timed[here, :width]).astype(BF)
        values[here, :] = (dot(near, w_value[:width, :]) + near_timed[here, width:]).astype(BF)
        hi, lo = split(query_2 * key.astype(F32))
        scores[here, :] = (dot(hi, heads) + dot(lo, heads)) * (1.0 / math.sqrt(head))
        return carry

    lax.fori_loop(0, neighbours // 2, score, 0)

    def slab(ref, k):
        return ref[k * events : (k + 1) * events, :]

    top = slab(scores, 0)
    for k in range(1, neighbours):
        top = jnp.maximum(top, slab(scores, k))
    total = jnp.zeros_like(top)
    for k in range(neighbours):
        raised = jnp.exp(slab(scores, k) - top)
        scores[k * events : (k + 1) * events, :] = raised
        total = total + raised
    scale = 1.0 / total
    attended = jnp.zeros_like(top)
    for k in range(neighbours):
        weight = (slab(scores, k) * scale).astype(BF).astype(F32)
        attended = attended + weight * slab(values, k).astype(F32)
    merged = dot(attended.astype(BF), w_merge[:width, :]) + dot(own, w_merge[width:, :])
    merged = jnp.maximum(merged + b_merge_in[...].reshape(1, -1), 0.0).astype(BF)
    out[...] = (dot(merged, w_out[...]) + b_out_in[...].reshape(1, -1)).astype(BF)

    result.wait()
    wait_bytes(others, ysend_sem)
    wait_bytes(reqr.at[pl.ds(0, domains - 1)], rsend_sem)
    for b in range(periods):
        wait_bytes(gsend.at[b, pl.ds(0, domains - 1)], gsend_sem.at[b])
    for step in range(nz // 2):
        for part in range(2):
            for up in (True, False):
                if moves(step, part, up):
                    pass_on(step, part, up).wait_send()
    wait_bytes(asked.at[pl.ds(0, GROUP - 1)], ask_send)
    for i in range(nz):
        wait_bytes(answers.at[i, pl.ds(0, GROUP - 1)], answer_send.at[i])


def on_device(*args):
    periods, domains = lax.axis_size("tm"), lax.axis_size("dom")
    nz = domains // GROUP
    nodes, width = args[0].shape
    neighbours, events = args[7].shape[1:]
    pairs = neighbours * events
    asked = domains * DCAP
    inputs = list(args)
    inputs[7] = args[7][0]
    inputs[8] = args[8][0]
    staged = [pltpu.VMEM(a.shape, a.dtype) for a in inputs]
    dma = pltpu.SemaphoreType.DMA
    updated, embedded = pl.pallas_call(
        functools.partial(whole_kernel, periods, domains),
        out_shape=(
            jax.ShapeDtypeStruct((nodes, width), F32),
            jax.ShapeDtypeStruct((events, width), BF),
        ),
        in_specs=[pl.BlockSpec(memory_space=pl.ANY)] * len(inputs),
        out_specs=[
            pl.BlockSpec(memory_space=pl.ANY),
            pl.BlockSpec(memory_space=pltpu.VMEM),
        ],
        scratch_shapes=staged
        + [
            pltpu.VMEM((nodes, width), F32),
            pltpu.VMEM((nz, GROUP, 1, CAP), jnp.int32),
            pltpu.VMEM((nodes, 2 * width), BF),
            pltpu.VMEM((16, 128), jnp.int32),
            pltpu.VMEM((periods, 16, 128), jnp.int32),
            pltpu.VMEM((domains, 1, 128), jnp.int32),
            pltpu.VMEM((domains, 1, 128), jnp.int32),
            pltpu.VMEM((periods, domains, 2 * DCAP, 128), BF),
            pltpu.VMEM((periods, domains, 2 * DCAP, 128), BF),
            pltpu.VMEM((2, asked, nodes), BF),
            pltpu.VMEM((2, events, nodes), BF),
            pltpu.VMEM((2, nodes, events), BF),
            pltpu.VMEM((2, events, events), BF),
            pltpu.VMEM((2, events, 3 * width), F32),
            pltpu.VMEM((2, nodes, 128), F32),
            pltpu.VMEM((2, events, 128), F32),
            pltpu.VMEM((nodes, width), BF),
            pltpu.VMEM((nz, nodes, width), BF),
            pltpu.VMEM((nz, GROUP, CAP, width), BF),
            pltpu.VMEM((nz, GROUP, CAP, width), BF),
            pltpu.VMEM((GROUP, nz, 1, CAP), jnp.int32),
            pltpu.VMEM((nz, GROUP * CAP, 128), BF),
            pltpu.VMEM((nz, GROUP * CAP, 128), BF),
            pltpu.VMEM((pairs, 128), BF),
            pltpu.VMEM((pairs, 128), BF),
            pltpu.VMEM((pairs, width), BF),
            pltpu.VMEM((pairs, 2 * width), F32),
            pltpu.VMEM((pairs, width), F32),
            pltpu.VMEM((pairs, width), BF),
            dma((len(inputs),)),
            dma(()),
            dma(()),
            dma(()),
            dma(()),
            dma(()),
            dma((periods,)),
            dma((periods,)),
            dma((nz // 2, 2)),
            dma((nz // 2, 2)),
            dma((nz // 2, 2)),
            dma((nz // 2, 2)),
            dma(()),
            dma(()),
            dma((nz,)),
            dma((nz,)),
        ],
        compiler_params=pltpu.CompilerParams(
            collective_id=0, has_side_effects=True, vmem_limit_bytes=60 * 2**20
        ),
        name="whole",
    )(*inputs)
    return (updated[None], embedded[None])


def solution(mesh):
    return jax.shard_map(
        on_device,
        mesh=mesh,
        in_specs=(
            P("dom", None),
            P("dom"),
            P("tm", "dom"),
            P("tm", "dom"),
            P("tm", "dom"),
            P("tm", "dom"),
            P("tm", "dom"),
            P("tm", None, "dom"),
            P("tm", None, "dom"),
            P(),
            P(),
            P(),
            P(),
            P(),
            P(),
            P(),
            P(),
            P(),
            P(),
            P(),
            P(),
            P(),
        ),
        out_specs=(P("tm", "dom", None), P("tm", "dom", None)),
        check_vma=False,
    )
```
